256 devices in a mesh: ctx: 64 (over y, z, core), chan: 4 (over x).
Axes of the slice: x: 4, y: 4, z: 8, core: 2. Of those that a mesh axis runs over, the one named last changes fastest.
Arguments:
- query_feat: bfloat16 [8192, 2048], P('ctx', 'chan'), may hold values from -6 to 6
- key_feat: bfloat16 [8192, 2048], P('ctx', 'chan'), may hold values from -6 to 6
- value_feat: bfloat16 [8192, 2048], P('ctx', 'chan'), may hold values from -6 to 6
- decay_rate: float32 [2048, 16], P('chan'), may hold values from 3.6621095e-05 to 0.03
- residue: float32 [2048, 16], P('chan'), may hold values from -0.12 to 0.12
- conv_skip: float32 [2048], P('chan'), may hold values from 0.1 to 1.9
- out_weight: bfloat16 [2048, 4096], P('chan'), may hold values from -0.125 to 0.125
- stream: bfloat16 [8192, 4096], P('ctx', 'chan'), may hold values from -6 to 6
- attn_query: bfloat16 [8192, 4096], P('ctx', 'chan'), may hold values from -8 to 8
- attn_key: bfloat16 [8192, 4096], P('ctx', 'chan'), may hold values from -8 to 8
- attn_value: bfloat16 [8192, 4096], P('ctx', 'chan'), may hold values from -6 to 6
- doc_start: int32 [8192], P('ctx'), may hold values from 0 to 8191, as said below
- read_mask: int32 [64, 4], P('ctx'), may hold values from 0 to 1, as said below
Outputs:
- mixed: bfloat16 [8192, 4096], P('ctx', 'chan')
- attended: bfloat16 [8192, 4096], P('ctx', 'chan')
The draws below stay inside these ranges and needn't reach their ends.
Inputs may be any that keep to these rules, and one draw needn't show every extreme that they name: doc_start[t] is the first position of the document that holds position t: never above t, never falling, the same for all positions of one document; documents are contiguous and hold 1 to 384 positions, and some document holds exactly 384. read_mask[b, k] is 1 exactly when b - k >= doc_start[b * 128] // 128; read_mask[b, 0] is always 1, and some row is all ones.
All inputs are finite; a program needn't handle non-finite values.
Results may differ from the reference program's by a relative error of at most 0.022.
Values may be sent and summed in bfloat16 or wider, within the bound.
No kernel may reach another device: no remote copies, remote signals or barrier semaphores. Data moves between devices by JAX's collectives and lax.ppermute only.
A program may use at most 64 MiB of HBM per device.

```python
import math
import jax
import jax.numpy as jnp
from jax import lax

D = 4096
CH = 2048
HEADS = 32
HD = 128
ORDER = 16
DOC_BLOCKS = 3
TOK_DEV = 128
SEQ = 8192
DOC_MOST = 384
N_CTX = 64


def doc_layout(key):
    first_key, second_key, third_key, fourth_key = jax.random.split(key, 4)
    short_lengths = jax.random.randint(first_key, (SEQ,), 8, 65)
    long_lengths = jax.random.randint(second_key, (SEQ,), DOC_MOST // 4, DOC_MOST + 1)
    coin_flips = jax.random.randint(third_key, (SEQ,), 0, 2)
    lengths = jnp.where(coin_flips == 1, short_lengths, long_lengths)
    lead_length = jax.random.randint(fourth_key, (), 1, TOK_DEV)
    lengths = lengths.at[0].set(lead_length).at[1].set(DOC_MOST)
    doc_starts = jnp.concatenate([jnp.zeros((1,), jnp.int32), jnp.cumsum(lengths)[:-1].astype(jnp.int32)])
    positions = jnp.arange(SEQ, dtype=jnp.int32)
    owner = jnp.searchsorted(doc_starts, positions, side='right') - 1
    starts_all = doc_starts[owner].astype(jnp.int32)
    return starts_all.at[SEQ - 1].set(SEQ - 1)


def draw_doc_start(key, part):
    return doc_layout(key)


def draw_read_mask(key, part):
    starts_all = doc_layout(key)
    first_block = starts_all[::TOK_DEV] // TOK_DEV
    block_ids = jnp.arange(N_CTX, dtype=jnp.int32)[:, None]
    back_ids = jnp.arange(DOC_BLOCKS + 1, dtype=jnp.int32)[None, :]
    return (block_ids - back_ids >= first_block[:, None]).astype(jnp.int32)


def draw_attn_query(key, part):
    key = jax.random.fold_in(key, 5)
    base = jnp.clip(jax.random.normal(key, (N_CTX, TOK_DEV, HEADS, HD)), -6.0, 6.0)
    return base.reshape(SEQ, HEADS * HD).astype(jnp.bfloat16)


def draw_attn_key(key, part):
    key = jax.random.fold_in(key, 7)
    base = jnp.clip(jax.random.normal(key, (N_CTX, TOK_DEV, HEADS, HD)), -6.0, 6.0)
    return base.reshape(SEQ, HEADS * HD).astype(jnp.bfloat16)


def block_scale(rng, dims, shards, smallest, top_value):
    loudness, own = 1.0, jax.random.fold_in(rng, 6)
    for axis_at, parts in shards:
        draws = jnp.exp(jax.random.uniform(jax.random.fold_in(own, axis_at), (parts,), jnp.float32, smallest / len(shards), top_value / len(shards)))
        loudness = loudness * jnp.repeat(draws, dims[axis_at] // parts).reshape([-1 if axis == axis_at else 1 for axis in range(len(dims))])
    return loudness


def bell_draw(rng, extent, spread, limit, pieces=(), held_as=jnp.bfloat16):
    drawn = jax.random.normal(rng, extent, jnp.float32) * spread
    if len(pieces) > 0:
        drawn = block_scale(rng, extent, pieces, -0.22, 0.18) * drawn
    return jnp.clip(drawn, min=-limit, max=limit).astype(held_as)


def setup_inputs(seed: int = 0) -> dict:
    streams_of = jax.random.split(jax.random.key(seed), 14)
    return {
        "query_feat": bell_draw(streams_of[0], (SEQ, CH), 1.0, 6.0, ((0, 64), (1, 4))),
        "key_feat": bell_draw(streams_of[1], (SEQ, CH), 1.0, 6.0, ((0, 64), (1, 4))),
        "value_feat": bell_draw(streams_of[2], (SEQ, CH), 1.0, 6.0, ((0, 64), (1, 4))),
        "decay_rate": jnp.clip(jnp.exp(math.log(0.03) - 6.7083282 * jax.random.uniform(streams_of[3], (CH, ORDER), jnp.float32) ** block_scale(streams_of[3], (CH, ORDER), ((0, 4),), -0.2, 0.2)), 3.662109520519152e-05, 0.03),
        "residue": bell_draw(streams_of[4], (CH, ORDER), 0.02, 0.12, ((0, 4),), jnp.float32),
        "conv_skip": jnp.clip(1.0 + 0.18 * jax.random.normal(streams_of[5], (CH,), jnp.float32), 0.1, 1.9),
        "out_weight": bell_draw(streams_of[6], (CH, D), CH ** -0.5, 0.125, ((0, 4),)),
        "stream": bell_draw(streams_of[7], (SEQ, D), 1.0, 6.0, ((0, 64), (1, 4))),
        "attn_query": draw_attn_query(jax.random.fold_in(streams_of[13], 71), 0),
        "attn_key": draw_attn_key(jax.random.fold_in(streams_of[13], 71), 0),
        "attn_value": bell_draw(streams_of[10], (SEQ, HEADS * HD), 1.0, 6.0, ((0, 64), (1, 4))),
        "doc_start": draw_doc_start(jax.random.fold_in(streams_of[13], 71), 0),
        "read_mask": draw_read_mask(jax.random.fold_in(streams_of[13], 71), 0),
    }


def reference(query_feat, key_feat, value_feat, decay_rate, residue, conv_skip, out_weight, stream, attn_query, attn_key, attn_value, doc_start, read_mask):
    product = key_feat.astype(jnp.float32) * value_feat.astype(jnp.float32)
    time_axis = jnp.arange(SEQ, dtype=jnp.float32)[:, None]
    kernel = jnp.zeros((SEQ, CH), jnp.float32)
    for order_index in range(ORDER):
        kernel = kernel + residue[:, order_index][None, :] * jnp.exp(-decay_rate[:, order_index][None, :] * time_axis)
    padded_len = 2 * SEQ
    spectrum = jnp.fft.rfft(product, n=padded_len, axis=0) * jnp.fft.rfft(kernel, n=padded_len, axis=0)
    convolved = jnp.fft.irfft(spectrum, n=padded_len, axis=0)[:SEQ].astype(jnp.float32)
    hyena = (query_feat.astype(jnp.float32) * (convolved + conv_skip[None, :] * product)).astype(jnp.bfloat16)
    mixed = (stream.astype(jnp.float32) + jnp.dot(hyena, out_weight, preferred_element_type=jnp.float32)).astype(jnp.bfloat16)

    window = (DOC_BLOCKS + 1) * TOK_DEV
    front_pad = jnp.zeros((DOC_BLOCKS * TOK_DEV, HEADS * HD), attn_key.dtype)
    key_padded = jnp.concatenate([front_pad, attn_key], axis=0)
    value_padded = jnp.concatenate([front_pad, attn_value], axis=0)

    def one_block(block_index):
        row_start = block_index * TOK_DEV
        queries = lax.dynamic_slice_in_dim(attn_query, row_start, TOK_DEV, 0).astype(jnp.float32).reshape(TOK_DEV, HEADS, HD)
        keys_here = lax.dynamic_slice_in_dim(key_padded, row_start, window, 0).astype(jnp.float32).reshape(window, HEADS, HD)
        values_here = lax.dynamic_slice_in_dim(value_padded, row_start, window, 0).astype(jnp.float32).reshape(window, HEADS, HD)
        key_pos = row_start - DOC_BLOCKS * TOK_DEV + jnp.arange(window, dtype=jnp.int32)
        query_pos = row_start + jnp.arange(TOK_DEV, dtype=jnp.int32)
        starts_here = lax.dynamic_slice_in_dim(doc_start, row_start, TOK_DEV, 0)
        mask_row = lax.dynamic_index_in_dim(read_mask, block_index, 0, keepdims=False)
        block_live = jnp.repeat(mask_row[::-1], TOK_DEV) == 1
        allowed = (key_pos[None, :] >= starts_here[:, None]) & (key_pos[None, :] <= query_pos[:, None]) & block_live[None, :]
        scores = jnp.einsum("qhd,khd->hqk", queries, keys_here) * (HD ** -0.5)
        scores = jnp.where(allowed[None], scores, -jnp.inf)
        top = jnp.max(scores, axis=-1, keepdims=True)
        weights = jnp.where(allowed[None], jnp.exp(scores - top), 0.0)
        total = jnp.sum(weights, axis=-1, keepdims=True)
        rounded = weights.astype(jnp.bfloat16)
        summed = jnp.einsum("hqk,khd->qhd", rounded.astype(jnp.float32), values_here)
        result = summed / jnp.transpose(total, (1, 0, 2))
        return result.reshape(TOK_DEV, HEADS * HD).astype(jnp.bfloat16)

    attended = lax.map(one_block, jnp.arange(SEQ // TOK_DEV, dtype=jnp.int32)).reshape(SEQ, HEADS * HD)
    return mixed, attended
```

```python
import math

import jax
import jax.numpy as jnp
from jax import lax
from jax.experimental import pallas as pl
from jax.experimental.pallas import tpu as pltpu
from jax.sharding import PartitionSpec as P

HD = 128
LANES = 128
DOC_BLOCKS = 3
VMEM = pltpu.VMEM


def whole(count):
    return [pl.BlockSpec(memory_space=VMEM) for _ in range(count)]


def shifted(value, axis, steps):
    count = lax.axis_size(axis)
    return lax.ppermute(value, axis, [(i, (i + steps) % count) for i in range(count)])


def core_swap(value):
    count = lax.axis_size("ctx")
    return lax.ppermute(value, "ctx", [(i, i ^ 1) for i in range(count)])


def room(mib):
    return pltpu.CompilerParams(vmem_limit_bytes=mib * 1024 * 1024)


def to_state_rows(source_ref, target_ref, groups):
    for g in range(groups):
        block = source_ref[:, g * LANES : (g + 1) * LANES]
        target_ref[pl.ds(g, block.shape[0], stride=groups), :] = block


def to_position_rows(product, target_ref, groups):
    rows = product.shape[0]
    for g in range(groups):
        block = product[:, g * LANES : (g + 1) * LANES]
        for half in range(2):
            target_ref[pl.ds(half * groups + g, rows, stride=2 * groups), :] = block


def states_kernel(
    key_ref, value_ref, decay_ref, keep_ref, send_ref, rates_ref, product_ref, state_ref
):
    groups = key_ref.shape[1] // LANES
    rows = key_ref.shape[0]
    to_state_rows(decay_ref, rates_ref, groups)
    product = key_ref[...].astype(jnp.float32) * value_ref[...].astype(jnp.float32)
    to_position_rows(product, product_ref, groups)
    count = rates_ref.shape[0] // 8
    steps = [jnp.exp(-rates_ref[8 * i : 8 * i + 8, :]) for i in range(count)]
    parts = 4
    span = rows // parts
    states = [[jnp.zeros((8, LANES), jnp.float32)] * count for _ in range(parts)]
    for t in range(span):
        for part in range(parts):
            row = 8 * (part * span + t)
            value = product_ref[row : row + 8, :]
            states[part] = [s * a + value for s, a in zip(states[part], steps)]
    for i in range(count):
        long_step = jnp.exp(-span * rates_ref[8 * i : 8 * i + 8, :])
        total = states[0][i]
        for part in range(1, parts):
            total = total * long_step + states[part][i]
        state_ref[8 * i : 8 * i + 8, :] = total
    core = lax.rem(lax.axis_index("ctx"), 2)
    half = state_ref.shape[0] // 2
    keep_ref[...] = state_ref[pl.ds(pl.multiple_of(core * half, half), half), :]
    send_ref[...] = state_ref[pl.ds(pl.multiple_of((1 - core) * half, half), half), :]


def pair_kernel(rows, keep_ref, got_ref, rates_ref, out_ref):
    core = lax.rem(lax.axis_index("ctx"), 2)
    half = keep_ref.shape[0]
    rates = rates_ref[pl.ds(pl.multiple_of(core * half, half), half), :]
    keep, got = keep_ref[...], got_ref[...]
    first = jnp.where(core == 0, keep, got)
    second = jnp.where(core == 0, got, keep)
    both = (first * jnp.exp(-rows * rates) + second).astype(out_ref.dtype)
    for i in range(out_ref.shape[0]):
        out_ref[i] = both


def carry_kernel(rows, all_ref, keep_ref, got_ref, rates_ref, mine_ref, other_ref):
    index = lax.axis_index("ctx")
    core = lax.rem(index, 2)
    chip = lax.div(index, 2)
    half = keep_ref.shape[0]
    rates = rates_ref[pl.ds(pl.multiple_of(core * half, half), half), :]
    step = jnp.exp(-2 * rows * rates)
    carry = jnp.zeros((half, LANES), jnp.float32)
    for i in range(all_ref.shape[0] - 1):
        carry = jnp.where(i < chip, carry * step + all_ref[i].astype(jnp.float32), carry)
    first = jnp.where(core == 0, keep_ref[...], got_ref[...])
    later = carry * jnp.exp(-rows * rates) + first
    mine_ref[...] = jnp.where(core == 0, carry, later)
    other_ref[...] = jnp.where(core == 0, later, carry)


def project_kernel(
    query_ref,
    key_ref,
    value_ref,
    rates_ref,
    residue_ref,
    skip_ref,
    mine_ref,
    other_ref,
    weight_hbm,
    own_ref,
    near_ref,
    far_ref,
    back_ref,
    product_ref,
    weights_ref,
    state_ref,
    conv_ref,
    weight_ref,
    sems,
):
    chan = lax.axis_index("chan")
    groups = key_ref.shape[1] // LANES
    rows = key_ref.shape[0]
    chans = weight_hbm.shape[1] // own_ref.shape[1]
    width = own_ref.shape[1]
    order = [2, 1, 3, 0]
    copies = []
    for slot, ahead in enumerate(order):
        column = pl.multiple_of(lax.rem(chan + ahead, chans) * width, width)
        copies.append(
            pltpu.make_async_copy(
                weight_hbm.at[:, pl.ds(column, width)], weight_ref.at[slot], sems.at[slot]
            )
        )
        copies[-1].start()
    to_state_rows(residue_ref, weights_ref, groups)
    product = key_ref[...].astype(jnp.float32) * value_ref[...].astype(jnp.float32)
    to_position_rows(product, product_ref, groups)
    core = lax.rem(lax.axis_index("ctx"), 2)
    half = mine_ref.shape[0]
    state_ref[pl.ds(pl.multiple_of(core * half, half), half), :] = mine_ref[...]
    state_ref[pl.ds(pl.multiple_of((1 - core) * half, half), half), :] = other_ref[...]
    count = rates_ref.shape[0] // 8
    steps = [jnp.exp(-rates_ref[8 * i : 8 * i + 8, :]) for i in range(count)]
    scale = [weights_ref[8 * i : 8 * i + 8, :] for i in range(count)]
    states = [state_ref[8 * i : 8 * i + 8, :] for i in range(count)]
    for t in range(rows):
        value = product_ref[8 * t : 8 * t + 8, :]
        states = [s * a + value for s, a in zip(states, steps)]
        terms = [s * w for s, w in zip(states, scale)]
        while len(terms) > 1:
            terms = [u + v for u, v in zip(terms[::2], terms[1::2])]
        conv_ref[8 * t : 8 * t + 8, :] = terms[0]
    blocks = []
    for g in range(groups):
        conv = (
            conv_ref[pl.ds(g, rows, stride=2 * groups), :]
            + conv_ref[pl.ds(groups + g, rows, stride=2 * groups), :]
        )
        lanes = slice(g * LANES, (g + 1) * LANES)
        skipped = skip_ref[:, lanes] * product[:, lanes]
        blocks.append(
            (query_ref[:, lanes].astype(jnp.float32) * (conv + skipped)).astype(jnp.bfloat16)
        )
    hyena = jnp.concatenate(blocks, axis=1)
    targets = [far_ref, near_ref, back_ref, own_ref]
    for slot, target in enumerate(targets):
        copies[slot].wait()
        target[...] = jnp.dot(
            hyena, weight_ref[slot], preferred_element_type=jnp.float32
        ).astype(target.dtype)


def attention_kernel(
    query_ref, key_ref, value_ref, one_ref, two_ref, three_ref, start_ref, read_ref, out_ref
):
    rows = query_ref.shape[0]
    base = lax.axis_index("ctx") * rows
    starts = jnp.broadcast_to(start_ref[...] - base, (rows, rows)).T
    query_pos = lax.broadcasted_iota(jnp.int32, (rows, rows), 0)
    key_pos = lax.broadcasted_iota(jnp.int32, (rows, rows), 1)
    allowed = []
    for back in range(DOC_BLOCKS, -1, -1):
        pos = key_pos - back * rows
        ok = (pos >= starts) & (read_ref[0, back] == 1)
        if back == 0:
            ok = ok & (pos <= query_pos)
        allowed.append(ok)
    mask = jnp.concatenate(allowed, axis=1)
    for head in range(query_ref.shape[1] // HD):
        cols = slice(head * HD, (head + 1) * HD)
        query = query_ref[:, cols]
        keys = [r[:rows, cols] for r in (three_ref, two_ref, one_ref)] + [key_ref[:, cols]]
        values = [r[rows:, cols] for r in (three_ref, two_ref, one_ref)] + [value_ref[:, cols]]
        keys = jnp.concatenate(keys, axis=0)
        values = jnp.concatenate(values, axis=0)
        scores = lax.dot_general(
            query, keys, (((1,), (1,)), ((), ())), preferred_element_type=jnp.float32
        )
        scores = jnp.where(mask, scores * HD ** (-0.5), -jnp.inf)
        top = jnp.max(scores, axis=1, keepdims=True)
        weights = jnp.exp(scores - top)
        total = jnp.sum(weights, axis=1, keepdims=True)
        summed = jnp.dot(weights.astype(jnp.bfloat16), values, preferred_element_type=jnp.float32)
        out_ref[:, cols] = (summed / total).astype(out_ref.dtype)


def shards(
    query_feat,
    key_feat,
    value_feat,
    decay_rate,
    residue,
    conv_skip,
    out_weight,
    stream,
    attn_query,
    attn_key,
    attn_value,
    doc_start,
    read_mask,
):
    ctx_count = lax.axis_size("ctx")
    rows, channels = query_feat.shape
    order = decay_rate.shape[1]
    state_rows = order * channels // LANES
    half = state_rows // 2
    chips = ctx_count // 2
    f32, bf16 = jnp.float32, jnp.bfloat16
    state_half = jax.ShapeDtypeStruct((half, LANES), f32)

    key_value = jnp.concatenate([attn_key, attn_value], axis=0)
    two_back = shifted(key_value, "ctx", 2)
    one_back = shifted(key_value, "ctx", 1)
    three_back = shifted(two_back, "ctx", 1)

    keep, send, rates = pl.pallas_call(
        states_kernel,
        out_shape=(state_half, state_half, jax.ShapeDtypeStruct((state_rows, LANES), f32)),
        in_specs=whole(3),
        out_specs=tuple(whole(3)),
        scratch_shapes=[VMEM((8 * rows, LANES), f32), VMEM((state_rows, LANES), f32)],
        compiler_params=room(4),
        name="filter_states",
    )(key_feat, value_feat, decay_rate.T)
    got = core_swap(send)
    spread = pl.pallas_call(
        lambda *refs: pair_kernel(rows, *refs),
        out_shape=jax.ShapeDtypeStruct((chips, half, LANES), bf16),
        in_specs=whole(3),
        out_specs=whole(1)[0],
        compiler_params=room(4),
        name="chip_states",
    )(keep, got, rates)
    groups = [list(range(core, ctx_count, 2)) for core in range(2)]
    spread = lax.all_to_all(spread, "ctx", 0, 0, axis_index_groups=groups)
    mine, other = pl.pallas_call(
        lambda *refs: carry_kernel(rows, *refs),
        out_shape=(state_half, state_half),
        in_specs=whole(4),
        out_specs=tuple(whole(2)),
        compiler_params=room(4),
        name="carried_states",
    )(spread, keep, got, rates)
    other = core_swap(other)

    width = out_weight.shape[1] // lax.axis_size("chan")
    piece = jax.ShapeDtypeStruct((rows, width), bf16)
    own, near, far, back = pl.pallas_call(
        project_kernel,
        out_shape=(jax.ShapeDtypeStruct((rows, width), f32), piece, piece, piece),
        in_specs=whole(8) + [pl.BlockSpec(memory_space=pl.ANY)],
        out_specs=tuple(whole(4)),
        scratch_shapes=[
            VMEM((8 * rows, LANES), f32),
            VMEM((state_rows, LANES), f32),
            VMEM((state_rows, LANES), f32),
            VMEM((8 * rows, LANES), f32),
            VMEM((4, channels, width), bf16),
            pltpu.SemaphoreType.DMA((4,)),
        ],
        compiler_params=room(12),
        name="project",
    )(
        query_feat,
        key_feat,
        value_feat,
        rates,
        residue.T,
        conv_skip.reshape(1, channels),
        mine,
        other,
        out_weight,
    )
    far = shifted(far, "chan", 2)
    near = shifted(near, "chan", 1)
    back = shifted(back, "chan", 3)

    attended = pl.pallas_call(
        attention_kernel,
        out_shape=jax.ShapeDtypeStruct(attn_query.shape, bf16),
        in_specs=whole(7) + [pl.BlockSpec(memory_space=pltpu.SMEM)],
        out_specs=whole(1)[0],
        compiler_params=room(12),
        name="attention",
    )(
        attn_query,
        attn_key,
        attn_value,
        one_back,
        two_back,
        three_back,
        doc_start.reshape(1, rows),
        read_mask,
    )
    summed = own + far.astype(f32) + near.astype(f32) + back.astype(f32)
    mixed = (stream.astype(f32) + summed).astype(bf16)
    return (mixed, attended)


def solution(mesh):
    in_specs = (
        P("ctx", "chan"),
        P("ctx", "chan"),
        P("ctx", "chan"),
        P("chan", None),
        P("chan", None),
        P("chan"),
        P("chan", None),
        P("ctx", "chan"),
        P("ctx", "chan"),
        P("ctx", "chan"),
        P("ctx", "chan"),
        P("ctx"),
        P("ctx", None),
    )
    out_specs = (P("ctx", "chan"), P("ctx", "chan"))
    return jax.shard_map(shards, mesh=mesh, in_specs=in_specs, out_specs=out_specs, check_vma=False)
```

```python
import math

import jax
import jax.numpy as jnp
from jax import lax
from jax.experimental import pallas as pl
from jax.experimental.pallas import tpu as pltpu
from jax.sharding import PartitionSpec as P

HD = 128
LANES = 128
DOC_BLOCKS = 3
VMEM = pltpu.VMEM


def whole(count):
    return [pl.BlockSpec(memory_space=VMEM) for _ in range(count)]


def in_hbm(count):
    return [pl.BlockSpec(memory_space=pltpu.HBM) for _ in range(count)]


def fixed(*values):
    return [pltpu.with_memory_space_constraint(value, pltpu.HBM) for value in values]


def shifted(value, axis, steps):
    count = lax.axis_size(axis)
    return lax.ppermute(value, axis, [(i, (i + steps) % count) for i in range(count)])


def core_swap(value):
    count = lax.axis_size("ctx")
    return lax.ppermute(value, "ctx", [(i, i ^ 1) for i in range(count)])


def room(mib):
    return pltpu.CompilerParams(vmem_limit_bytes=mib * 1024 * 1024)


def to_state_rows(source_ref, target_ref, groups):
    for g in range(groups):
        block = source_ref[:, g * LANES : (g + 1) * LANES]
        target_ref[pl.ds(g, block.shape[0], stride=groups), :] = block


def to_position_rows(product, target_ref, groups):
    rows = product.shape[0]
    for g in range(groups):
        block = product[:, g * LANES : (g + 1) * LANES]
        for half in range(2):
            target_ref[pl.ds(half * groups + g, rows, stride=2 * groups), :] = block


def load(pairs, sems):
    copies = [
        pltpu.make_async_copy(source, target, sems.at[i])
        for i, (source, target) in enumerate(pairs)
    ]
    for copy in copies:
        copy.start()
    return copies


def half_rows(ref, part):
    half = ref.shape[0] // 2
    return ref[pl.ds(pl.multiple_of(part * half, half), half), :]


def states_kernel(
    key_hbm,
    value_hbm,
    decay_hbm,
    attn_key_hbm,
    attn_value_hbm,
    keep_ref,
    send_ref,
    rates_ref,
    block_ref,
    key_ref,
    value_ref,
    decay_ref,
    product_ref,
    all_rates_ref,
    state_ref,
    sems,
):
    copies = load(
        [
            (decay_hbm, decay_ref),
            (key_hbm, key_ref),
            (value_hbm, value_ref),
            (attn_key_hbm, block_ref.at[: attn_key_hbm.shape[0]]),
            (attn_value_hbm, block_ref.at[attn_key_hbm.shape[0] :]),
        ],
        sems,
    )
    groups = key_ref.shape[1] // LANES
    rows = key_ref.shape[0]
    copies[0].wait()
    to_state_rows(decay_ref, all_rates_ref, groups)
    count = all_rates_ref.shape[0] // 8
    steps = [jnp.exp(-all_rates_ref[8 * i : 8 * i + 8, :]) for i in range(count)]
    copies[1].wait()
    copies[2].wait()
    product = key_ref[...].astype(jnp.float32) * value_ref[...].astype(jnp.float32)
    to_position_rows(product, product_ref, groups)
    parts = 4
    span = rows // parts
    states = [[jnp.zeros((8, LANES), jnp.float32)] * count for _ in range(parts)]
    for t in range(span):
        for part in range(parts):
            row = 8 * (part * span + t)
            value = product_ref[row : row + 8, :]
            states[part] = [s * a + value for s, a in zip(states[part], steps)]
    for i in range(count):
        long_step = jnp.exp(-span * all_rates_ref[8 * i : 8 * i + 8, :])
        total = states[0][i]
        for part in range(1, parts):
            total = total * long_step + states[part][i]
        state_ref[8 * i : 8 * i + 8, :] = total
    core = lax.rem(lax.axis_index("ctx"), 2)
    keep_ref[...] = half_rows(state_ref, core)
    send_ref[...] = half_rows(state_ref, 1 - core)
    rates_ref[...] = half_rows(all_rates_ref, core)
    copies[3].wait()
    copies[4].wait()


def carry_kernel(rows, all_ref, keep_ref, got_ref, rates_ref, *refs):
    mine_ref, other_ref = refs[-2:]
    index = lax.axis_index("ctx")
    core = lax.rem(index, 2)
    chip = lax.div(index, 2)
    half = keep_ref.shape[0]
    rates = rates_ref[...]
    step = jnp.exp(-2 * rows * rates)
    carry = jnp.zeros((half, LANES), jnp.float32)
    for i in range(all_ref.shape[0] - 1):
        carry = jnp.where(i < chip, carry * step + all_ref[i].astype(jnp.float32), carry)
    first = jnp.where(core == 0, keep_ref[...], got_ref[...])
    later = carry * jnp.exp(-rows * rates) + first
    mine_ref[...] = jnp.where(core == 0, carry, later)
    other_ref[...] = jnp.where(core == 0, later, carry)


def local_kernel(
    after_ref,
    key_hbm,
    value_hbm,
    decay_hbm,
    residue_hbm,
    query_hbm,
    skip_hbm,
    weight_hbm,
    query_ref,
    base_ref,
    steps_ref,
    scale_ref,
    far_ref,
    near_ref,
    key_ref,
    value_ref,
    decay_ref,
    residue_ref,
    skip_ref,
    product_ref,
    conv_ref,
    sems,
):
    copies = load(
        [
            (decay_hbm, decay_ref),
            (residue_hbm, residue_ref),
            (key_hbm, key_ref),
            (value_hbm, value_ref),
            (query_hbm, query_ref),
            (skip_hbm, skip_ref),
            *weight_pairs(weight_hbm, 2, far_ref),
            *weight_pairs(weight_hbm, 1, near_ref),
        ],
        sems,
    )
    for copy in copies[:-8]:
        copy.wait()
    groups = key_ref.shape[1] // LANES
    rows = key_ref.shape[0]
    to_state_rows(decay_ref, steps_ref, groups)
    to_state_rows(residue_ref, scale_ref, groups)
    steps_ref[...] = jnp.exp(-steps_ref[...])
    product = key_ref[...].astype(jnp.float32) * value_ref[...].astype(jnp.float32)
    to_position_rows(product, product_ref, groups)
    count = steps_ref.shape[0] // 8
    steps = [steps_ref[8 * i : 8 * i + 8, :] for i in range(count)]
    scale = [scale_ref[8 * i : 8 * i + 8, :] for i in range(count)]
    states = [jnp.zeros((8, LANES), jnp.float32)] * count
    for t in range(rows):
        value = product_ref[8 * t : 8 * t + 8, :]
        states = [s * a + value for s, a in zip(states, steps)]
        conv_ref[8 * t : 8 * t + 8, :] = tree_sum([s * w for s, w in zip(states, scale)])
    for g in range(groups):
        lanes = slice(g * LANES, (g + 1) * LANES)
        base_ref[:, lanes] = (
            from_position_rows(conv_ref, g, groups) + skip_ref[:, lanes] * product[:, lanes]
        )
    for copy in copies[-8:]:
        copy.wait()


def tree_sum(terms):
    while len(terms) > 1:
        terms = [u + v for u, v in zip(terms[::2], terms[1::2])]
    return terms[0]


def from_position_rows(source_ref, g, groups):
    rows = source_ref.shape[0] // (2 * groups)
    return (
        source_ref[pl.ds(g, rows, stride=2 * groups), :]
        + source_ref[pl.ds(groups + g, rows, stride=2 * groups), :]
    )


def gate_kernel(
    query_ref,
    base_ref,
    steps_ref,
    scale_ref,
    mine_ref,
    other_ref,
    far_weight_ref,
    near_weight_ref,
    weight_hbm,
    hyena_ref,
    far_ref,
    near_ref,
    back_ref,
    state_ref,
    conv_ref,
    back_weight_ref,
    sems,
):
    copies = load(weight_pairs(weight_hbm, 3, back_weight_ref), sems)
    rows = query_ref.shape[0]
    groups = query_ref.shape[1] // LANES
    core = lax.rem(lax.axis_index("ctx"), 2)
    half = mine_ref.shape[0]
    state_ref[pl.ds(pl.multiple_of(core * half, half), half), :] = mine_ref[...]
    state_ref[pl.ds(pl.multiple_of((1 - core) * half, half), half), :] = other_ref[...]
    count = steps_ref.shape[0] // 8
    steps = [steps_ref[8 * i : 8 * i + 8, :] for i in range(count)]
    states = [
        state_ref[8 * i : 8 * i + 8, :] * scale_ref[8 * i : 8 * i + 8, :] for i in range(count)
    ]
    for t in range(rows):
        states = [s * a for s, a in zip(states, steps)]
        conv_ref[8 * t : 8 * t + 8, :] = tree_sum(states)
    for g in range(groups):
        lanes = slice(g * LANES, (g + 1) * LANES)
        conv = from_position_rows(conv_ref, g, groups) + base_ref[:, lanes]
        hyena_ref[:, lanes] = (query_ref[:, lanes].astype(jnp.float32) * conv).astype(
            hyena_ref.dtype
        )
    pairs = ((far_weight_ref, far_ref), (near_weight_ref, near_ref), (back_weight_ref, back_ref))
    for weight_ref, target in pairs:
        if target is back_ref:
            for copy in copies:
                copy.wait()
        target[...] = jnp.dot(
            hyena_ref[...], weight_ref[...], preferred_element_type=jnp.float32
        ).astype(target.dtype)


def weight_pairs(weight_hbm, ahead, target_ref):
    source = weight_columns(weight_hbm, ahead, target_ref.shape[1])
    quarter = target_ref.shape[0] // 4
    rows = [slice(i * quarter, (i + 1) * quarter) for i in range(4)]
    return [(source.at[part, :], target_ref.at[part, :]) for part in rows]


def weight_columns(weight_hbm, ahead, width):
    chan, chans = lax.axis_index("chan"), weight_hbm.shape[1] // width
    column = pl.multiple_of(lax.rem(chan + ahead, chans) * width, width)
    return weight_hbm.at[:, pl.ds(column, width)]


def own_kernel(hyena_ref, weight_hbm, stream_hbm, own_ref, weight_ref, stream_ref, sems):
    copies = load(
        [*weight_pairs(weight_hbm, 0, weight_ref), (stream_hbm, stream_ref)],
        sems,
    )
    for copy in copies:
        copy.wait()
    own_ref[...] = stream_ref[...].astype(jnp.float32) + jnp.dot(
        hyena_ref[...], weight_ref[...], preferred_element_type=jnp.float32
    )


def finish_kernel(own_ref, far_ref, near_ref, back_ref, after_ref, out_ref):
    total = own_ref[...]
    for ref in (far_ref, near_ref, back_ref):
        total = total + ref[...].astype(jnp.float32)
    out_ref[...] = total.astype(out_ref.dtype)


def attention_kernel(
    query_hbm,
    block_hbm,
    one_hbm,
    two_hbm,
    three_hbm,
    start_ref,
    read_ref,
    out_ref,
    query_ref,
    block_ref,
    one_ref,
    two_ref,
    three_ref,
    sems,
):
    copies = load(
        [
            (query_hbm, query_ref),
            (block_hbm, block_ref),
            (one_hbm, one_ref),
            (two_hbm, two_ref),
            (three_hbm, three_ref),
        ],
        sems,
    )
    rows = query_ref.shape[0]
    base = lax.axis_index("ctx") * rows
    starts = jnp.broadcast_to(start_ref[...] - base, (rows, rows)).T
    query_pos = lax.broadcasted_iota(jnp.int32, (rows, rows), 0)
    key_pos = lax.broadcasted_iota(jnp.int32, (rows, rows), 1)
    allowed = []
    for back in range(DOC_BLOCKS, -1, -1):
        pos = key_pos - back * rows
        ok = (pos >= starts) & (read_ref[0, back] == 1)
        if back == 0:
            ok = ok & (pos <= query_pos)
        allowed.append(ok)
    mask = jnp.concatenate(allowed, axis=1)
    for copy in copies:
        copy.wait()
    for head in range(query_ref.shape[1] // HD):
        cols = slice(head * HD, (head + 1) * HD)
        query = query_ref[:, cols]
        blocks = (three_ref, two_ref, one_ref, block_ref)
        keys = jnp.concatenate([ref[:rows, cols] for ref in blocks], axis=0)
        values = jnp.concatenate([ref[rows:, cols] for ref in blocks], axis=0)
        scores = lax.dot_general(
            query, keys, (((1,), (1,)), ((), ())), preferred_element_type=jnp.float32
        )
        scores = jnp.where(mask, scores * HD ** (-0.5), -jnp.inf)
        top = jnp.max(scores, axis=1, keepdims=True)
        weights = jnp.exp(scores - top)
        total = jnp.sum(weights, axis=1, keepdims=True)
        summed = jnp.dot(weights.astype(jnp.bfloat16), values, preferred_element_type=jnp.float32)
        out_ref[:, cols] = (summed / total).astype(out_ref.dtype)


def shards(
    query_feat,
    key_feat,
    value_feat,
    decay_rate,
    residue,
    conv_skip,
    out_weight,
    stream,
    attn_query,
    attn_key,
    attn_value,
    doc_start,
    read_mask,
):
    rows, channels = query_feat.shape
    order = decay_rate.shape[1]
    state_rows = order * channels // LANES
    f32, bf16 = jnp.float32, jnp.bfloat16
    ctx_count = lax.axis_size("ctx")
    core = lax.axis_index("ctx") % 2
    half = state_rows // 2
    state = jax.ShapeDtypeStruct((state_rows, LANES), f32)
    state_half = jax.ShapeDtypeStruct((half, LANES), f32)

    keep, send, rates, block = pl.pallas_call(
        states_kernel,
        out_shape=(
            state_half,
            state_half,
            state_half,
            jax.ShapeDtypeStruct((2 * rows, attn_key.shape[1]), bf16),
        ),
        in_specs=in_hbm(5),
        out_specs=tuple(whole(4)),
        scratch_shapes=[
            VMEM((rows, channels), bf16),
            VMEM((rows, channels), bf16),
            VMEM((order, channels), f32),
            VMEM((8 * rows, LANES), f32),
            VMEM((state_rows, LANES), f32),
            VMEM((state_rows, LANES), f32),
            pltpu.SemaphoreType.DMA((5,)),
        ],
        compiler_params=room(4),
        name="filter_states",
    )(*fixed(key_feat, value_feat, decay_rate.T, attn_key, attn_value))
    block_2 = shifted(block, "ctx", 2)
    block_3 = shifted(block_2, "ctx", 1)
    block_1 = core_swap(jnp.where(core == 0, block, block_2))
    got = core_swap(send)
    first = jnp.where(core == 0, keep, got)
    second = jnp.where(core == 0, got, keep)
    both = (first * jnp.exp(-rows * rates) + second).astype(bf16)
    groups = [list(range(c, ctx_count, 2)) for c in range(2)]
    spread = lax.all_to_all(
        jnp.broadcast_to(both, (ctx_count // 2, half, LANES)),
        "ctx",
        0,
        0,
        axis_index_groups=groups,
    )

    width = out_weight.shape[1] // lax.axis_size("chan")
    columns = jax.ShapeDtypeStruct((channels, width), bf16)
    query, base, steps, scale, *weights = pl.pallas_call(
        local_kernel,
        out_shape=(
            jax.ShapeDtypeStruct((rows, channels), bf16),
            jax.ShapeDtypeStruct((rows, channels), f32),
            state,
            state,
            columns,
            columns,
        ),
        in_specs=whole(1) + in_hbm(7),
        out_specs=tuple(whole(6)),
        scratch_shapes=[
            VMEM((rows, channels), bf16),
            VMEM((rows, channels), bf16),
            VMEM((order, channels), f32),
            VMEM((order, channels), f32),
            VMEM((1, channels), f32),
            VMEM((8 * rows, LANES), f32),
            VMEM((8 * rows, LANES), f32),
            pltpu.SemaphoreType.DMA((14,)),
        ],
        compiler_params=room(6),
        cost_estimate=pl.CostEstimate(flops=0, bytes_accessed=8 * 1024 * 1024, transcendentals=0),
        name="local_part",
    )(
        got,
        *fixed(
            key_feat,
            value_feat,
            decay_rate.T,
            residue.T,
            query_feat,
            conv_skip.reshape(1, channels),
            out_weight,
        ),
    )
    mine, other = pl.pallas_call(
        lambda *refs: carry_kernel(rows, *refs),
        out_shape=(state_half, state_half),
        in_specs=whole(4) + [pl.BlockSpec(memory_space=pl.ANY)],
        out_specs=tuple(whole(2)),
        compiler_params=room(4),
        name="carried_states",
    )(spread, keep, got, rates, steps)
    other = core_swap(other)

    piece = jax.ShapeDtypeStruct((rows, width), bf16)
    hyena, far, near, back = pl.pallas_call(
        gate_kernel,
        out_shape=(jax.ShapeDtypeStruct((rows, channels), bf16), piece, piece, piece),
        in_specs=whole(8) + in_hbm(1),
        out_specs=tuple(whole(4)),
        scratch_shapes=[
            VMEM((state_rows, LANES), f32),
            VMEM((8 * rows, LANES), f32),
            VMEM((channels, width), bf16),
            pltpu.SemaphoreType.DMA((4,)),
        ],
        compiler_params=room(4),
        name="gate",
    )(query, base, steps, scale, mine, other, *weights, *fixed(out_weight))
    own = pl.pallas_call(
        own_kernel,
        out_shape=jax.ShapeDtypeStruct((rows, width), f32),
        in_specs=whole(1) + in_hbm(2),
        out_specs=whole(1)[0],
        scratch_shapes=[
            VMEM((channels, width), bf16),
            VMEM((rows, width), bf16),
            pltpu.SemaphoreType.DMA((5,)),
        ],
        compiler_params=room(8),
        name="own",
    )(hyena, *fixed(out_weight, stream))
    far = shifted(far, "chan", 2)
    near = shifted(near, "chan", 1)
    back = shifted(back, "chan", 3)

    attended = pl.pallas_call(
        attention_kernel,
        out_shape=jax.ShapeDtypeStruct(attn_query.shape, bf16),
        in_specs=in_hbm(5) + whole(1) + [pl.BlockSpec(memory_space=pltpu.SMEM)],
        out_specs=whole(1)[0],
        scratch_shapes=[VMEM(attn_query.shape, bf16)]
        + [VMEM((2 * rows, attn_query.shape[1]), bf16)] * 4
        + [pltpu.SemaphoreType.DMA((5,))],
        compiler_params=room(8),
        name="attention",
    )(
        *fixed(attn_query, block, block_1, block_2, block_3),
        doc_start.reshape(1, rows),
        read_mask,
    )
    mixed = pl.pallas_call(
        finish_kernel,
        out_shape=jax.ShapeDtypeStruct(stream.shape, bf16),
        in_specs=whole(4) + [pl.BlockSpec(memory_space=pl.ANY)],
        out_specs=whole(1)[0],
        compiler_params=room(4),
        name="finish",
    )(own, far, near, back, *fixed(attended))
    return (mixed, attended)


def solution(mesh):
    in_specs = (
        P("ctx", "chan"),
        P("ctx", "chan"),
        P("ctx", "chan"),
        P("chan", None),
        P("chan", None),
        P("chan"),
        P("chan", None),
        P("ctx", "chan"),
        P("ctx", "chan"),
        P("ctx", "chan"),
        P("ctx", "chan"),
        P("ctx"),
        P("ctx", None),
    )
    out_specs = (P("ctx", "chan"), P("ctx", "chan"))
    return jax.shard_map(shards, mesh=mesh, in_specs=in_specs, out_specs=out_specs, check_vma=False)
```

```python
import math

import jax
import jax.numpy as jnp
from jax import lax
from jax.experimental import pallas as pl
from jax.experimental.pallas import tpu as pltpu
from jax.sharding import PartitionSpec as P

HD = 128
LANES = 128
DOC_BLOCKS = 3
VMEM = pltpu.VMEM


def whole(count):
    return [pl.BlockSpec(memory_space=VMEM) for _ in range(count)]


def in_hbm(count):
    return [pl.BlockSpec(memory_space=pltpu.HBM) for _ in range(count)]


def fixed(*values):
    return [pltpu.with_memory_space_constraint(value, pltpu.HBM) for value in values]


def shifted(value, axis, steps):
    count = lax.axis_size(axis)
    return lax.ppermute(value, axis, [(i, (i + steps) % count) for i in range(count)])


def core_swap(value):
    count = lax.axis_size("ctx")
    return lax.ppermute(value, "ctx", [(i, i ^ 1) for i in range(count)])


def room(mib):
    return pltpu.CompilerParams(vmem_limit_bytes=mib * 1024 * 1024)


def to_state_rows(source_ref, target_ref, groups):
    for g in range(groups):
        block = source_ref[:, g * LANES : (g + 1) * LANES]
        target_ref[pl.ds(g, block.shape[0], stride=groups), :] = block


def to_position_rows(product, target_ref, groups):
    rows = product.shape[0]
    for g in range(groups):
        block = product[:, g * LANES : (g + 1) * LANES]
        for half in range(2):
            target_ref[pl.ds(half * groups + g, rows, stride=2 * groups), :] = block


def load(pairs, sems):
    copies = [
        pltpu.make_async_copy(source, target, sems.at[i])
        for i, (source, target) in enumerate(pairs)
    ]
    for copy in copies:
        copy.start()
    return copies


def half_rows(ref, part):
    half = ref.shape[0] // 2
    return ref[pl.ds(pl.multiple_of(part * half, half), half), :]


def states_kernel(
    key_hbm,
    value_hbm,
    decay_hbm,
    attn_key_hbm,
    attn_value_hbm,
    weight_hbm,
    keep_ref,
    send_ref,
    rates_ref,
    block_ref,
    far_ref,
    key_ref,
    value_ref,
    decay_ref,
    product_ref,
    all_rates_ref,
    state_ref,
    sems,
):
    core = lax.rem(lax.axis_index("ctx"), 2)
    far_source = weight_columns(weight_hbm, 2, far_ref.shape[1])
    far_rows = pl.ds(pl.multiple_of(core * far_ref.shape[0], far_ref.shape[0]), far_ref.shape[0])
    copies = load(
        [
            (decay_hbm, decay_ref),
            (key_hbm, key_ref),
            (value_hbm, value_ref),
            (far_source.at[far_rows, :], far_ref),
            (attn_key_hbm, block_ref.at[: attn_key_hbm.shape[0]]),
            (attn_value_hbm, block_ref.at[attn_key_hbm.shape[0] :]),
        ],
        sems,
    )
    groups = key_ref.shape[1] // LANES
    rows = key_ref.shape[0]
    copies[0].wait()
    to_state_rows(decay_ref, all_rates_ref, groups)
    count = all_rates_ref.shape[0] // 8
    steps = [jnp.exp(-all_rates_ref[8 * i : 8 * i + 8, :]) for i in range(count)]
    copies[1].wait()
    copies[2].wait()
    product = key_ref[...].astype(jnp.float32) * value_ref[...].astype(jnp.float32)
    to_position_rows(product, product_ref, groups)
    parts = 4
    span = rows // parts
    states = [[jnp.zeros((8, LANES), jnp.float32)] * count for _ in range(parts)]
    for t in range(span):
        for part in range(parts):
            row = 8 * (part * span + t)
            value = product_ref[row : row + 8, :]
            states[part] = [s * a + value for s, a in zip(states[part], steps)]
    for i in range(count):
        long_step = jnp.exp(-span * all_rates_ref[8 * i : 8 * i + 8, :])
        total = states[0][i]
        for part in range(1, parts):
            total = total * long_step + states[part][i]
        state_ref[8 * i : 8 * i + 8, :] = total
    keep_ref[...] = half_rows(state_ref, core)
    send_ref[...] = half_rows(state_ref, 1 - core)
    rates_ref[...] = half_rows(all_rates_ref, core)
    for copy in copies[3:]:
        copy.wait()


def carry_kernel(rows, all_ref, keep_ref, got_ref, rates_ref, *refs):
    mine_ref, other_ref = refs[-2:]
    index = lax.axis_index("ctx")
    core = lax.rem(index, 2)
    chip = lax.div(index, 2)
    half = keep_ref.shape[0]
    rates = rates_ref[...]
    step = jnp.exp(-2 * rows * rates)
    carry = jnp.zeros((half, LANES), jnp.float32)
    for i in range(all_ref.shape[0] - 1):
        carry = jnp.where(i < chip, carry * step + all_ref[i].astype(jnp.float32), carry)
    first = jnp.where(core == 0, keep_ref[...], got_ref[...])
    later = carry * jnp.exp(-rows * rates) + first
    mine_ref[...] = jnp.where(core == 0, carry, later)
    other_ref[...] = jnp.where(core == 0, later, carry)


def local_kernel(
    after_ref,
    key_hbm,
    value_hbm,
    decay_hbm,
    residue_hbm,
    query_hbm,
    skip_hbm,
    weight_hbm,
    query_ref,
    base_ref,
    steps_ref,
    scale_ref,
    near_ref,
    back_ref,
    key_ref,
    value_ref,
    decay_ref,
    residue_ref,
    skip_ref,
    product_ref,
    conv_ref,
    sems,
):
    copies = load(
        [
            (decay_hbm, decay_ref),
            (residue_hbm, residue_ref),
            (key_hbm, key_ref),
            (value_hbm, value_ref),
            (query_hbm, query_ref),
            (skip_hbm, skip_ref),
            *weight_pairs(weight_hbm, 1, near_ref),
            *weight_pairs(weight_hbm, 3, back_ref),
        ],
        sems,
    )
    for copy in copies[:-8]:
        copy.wait()
    groups = key_ref.shape[1] // LANES
    rows = key_ref.shape[0]
    to_state_rows(decay_ref, steps_ref, groups)
    to_state_rows(residue_ref, scale_ref, groups)
    steps_ref[...] = jnp.exp(-steps_ref[...])
    product = key_ref[...].astype(jnp.float32) * value_ref[...].astype(jnp.float32)
    to_position_rows(product, product_ref, groups)
    count = steps_ref.shape[0] // 8
    steps = [steps_ref[8 * i : 8 * i + 8, :] for i in range(count)]
    scale = [scale_ref[8 * i : 8 * i + 8, :] for i in range(count)]
    states = [jnp.zeros((8, LANES), jnp.float32)] * count
    for t in range(rows):
        value = product_ref[8 * t : 8 * t + 8, :]
        states = [s * a + value for s, a in zip(states, steps)]
        conv_ref[8 * t : 8 * t + 8, :] = tree_sum([s * w for s, w in zip(states, scale)])
    for g in range(groups):
        lanes = slice(g * LANES, (g + 1) * LANES)
        base_ref[:, lanes] = (
            from_position_rows(conv_ref, g, groups) + skip_ref[:, lanes] * product[:, lanes]
        )
    for copy in copies[-8:]:
        copy.wait()


def tree_sum(terms):
    while len(terms) > 1:
        terms = [u + v for u, v in zip(terms[::2], terms[1::2])]
    return terms[0]


def from_position_rows(source_ref, g, groups):
    rows = source_ref.shape[0] // (2 * groups)
    return (
        source_ref[pl.ds(g, rows, stride=2 * groups), :]
        + source_ref[pl.ds(groups + g, rows, stride=2 * groups), :]
    )


def gate_kernel(
    query_ref,
    base_ref,
    steps_ref,
    scale_ref,
    mine_ref,
    other_ref,
    hyena_ref,
    state_ref,
    conv_ref,
):
    rows = query_ref.shape[0]
    groups = query_ref.shape[1] // LANES
    core = lax.rem(lax.axis_index("ctx"), 2)
    half = mine_ref.shape[0]
    state_ref[pl.ds(pl.multiple_of(core * half, half), half), :] = mine_ref[...]
    state_ref[pl.ds(pl.multiple_of((1 - core) * half, half), half), :] = other_ref[...]
    count = steps_ref.shape[0] // 8
    steps = [steps_ref[8 * i : 8 * i + 8, :] for i in range(count)]
    states = [
        state_ref[8 * i : 8 * i + 8, :] * scale_ref[8 * i : 8 * i + 8, :] for i in range(count)
    ]
    for t in range(rows):
        states = [s * a for s, a in zip(states, steps)]
        conv_ref[8 * t : 8 * t + 8, :] = tree_sum(states)
    for g in range(groups):
        lanes = slice(g * LANES, (g + 1) * LANES)
        conv = from_position_rows(conv_ref, g, groups) + base_ref[:, lanes]
        hyena_ref[:, lanes] = (query_ref[:, lanes].astype(jnp.float32) * conv).astype(
            hyena_ref.dtype
        )


def near_kernel(hyena_ref, near_weight_ref, back_weight_ref, near_ref, back_ref):
    for weight_ref, target in ((near_weight_ref, near_ref), (back_weight_ref, back_ref)):
        target[...] = jnp.dot(
            hyena_ref[...], weight_ref[...], preferred_element_type=jnp.float32
        ).astype(target.dtype)


def weight_pairs(weight_hbm, ahead, target_ref):
    source = weight_columns(weight_hbm, ahead, target_ref.shape[1])
    quarter = target_ref.shape[0] // 4
    rows = [slice(i * quarter, (i + 1) * quarter) for i in range(4)]
    return [(source.at[part, :], target_ref.at[part, :]) for part in rows]


def weight_columns(weight_hbm, ahead, width):
    chan, chans = lax.axis_index("chan"), weight_hbm.shape[1] // width
    column = pl.multiple_of(lax.rem(chan + ahead, chans) * width, width)
    return weight_hbm.at[:, pl.ds(column, width)]


def far_kernel(own_ref, far_ref, weight_ref, out_ref):
    out_ref[...] = own_ref[...] + jnp.dot(
        far_ref[...], weight_ref[...], preferred_element_type=jnp.float32
    )


def finish_kernel(own_ref, near_ref, back_ref, after_ref, out_ref):
    total = own_ref[...] + near_ref[...].astype(jnp.float32) + back_ref[...].astype(jnp.float32)
    out_ref[...] = total.astype(out_ref.dtype)


def attention_kernel(
    query_hbm,
    block_hbm,
    one_hbm,
    two_hbm,
    three_hbm,
    weight_hbm,
    stream_hbm,
    half_hbm,
    other_hbm,
    hyena_ref,
    start_ref,
    read_ref,
    out_ref,
    own_ref,
    far_ref,
    query_ref,
    block_ref,
    one_ref,
    two_ref,
    three_ref,
    weight_ref,
    stream_ref,
    sems,
    own_sems,
):
    core = lax.rem(lax.axis_index("ctx"), 2)
    sources = (query_hbm, block_hbm, one_hbm, two_hbm, three_hbm)
    targets = (query_ref, block_ref, one_ref, two_ref, three_ref)
    chunk = query_ref.shape[1] // 4
    waits = []
    for i in range(4):
        cols = slice(i * chunk, (i + 1) * chunk)
        pairs = [(source.at[:, cols], target.at[:, cols]) for source, target in zip(sources, targets)]
        waits.append(load(pairs, sems.at[i]))
    half = half_hbm.shape[0]
    pairs = [*weight_pairs(weight_hbm, 0, weight_ref), (stream_hbm, stream_ref)]
    for part, source in ((core, half_hbm), (1 - core, other_hbm)):
        part_rows = pl.ds(pl.multiple_of(part * half, half), half)
        pairs.append((source, far_ref.at[part_rows, :]))
    own_copies = load(pairs, own_sems)
    rows = query_ref.shape[0]
    base = lax.axis_index("ctx") * rows
    starts = jnp.broadcast_to(start_ref[...] - base, (rows, rows)).T
    query_pos = lax.broadcasted_iota(jnp.int32, (rows, rows), 0)
    key_pos = lax.broadcasted_iota(jnp.int32, (rows, rows), 1)
    allowed = []
    for back in range(DOC_BLOCKS, -1, -1):
        pos = key_pos - back * rows
        ok = (pos >= starts) & (read_ref[0, back] == 1)
        if back == 0:
            ok = ok & (pos <= query_pos)
        allowed.append(ok)
    mask = jnp.concatenate(allowed, axis=1)
    scale = math.log2(math.e) * HD ** (-0.5)
    blocks = (three_ref, two_ref, one_ref, block_ref)
    for head in range(query_ref.shape[1] // HD):
        if head * HD % chunk == 0:
            for copy in waits[head * HD // chunk]:
                copy.wait()
        cols = slice(head * HD, (head + 1) * HD)
        keys = jnp.concatenate([ref[:rows, cols] for ref in blocks], axis=0)
        values = jnp.concatenate([ref[rows:, cols] for ref in blocks], axis=0)
        scores = lax.dot_general(
            query_ref[:, cols], keys, (((1,), (1,)), ((), ())), preferred_element_type=jnp.float32
        )
        scores = jnp.where(mask, scores * scale, -jnp.inf)
        top = jnp.max(scores, axis=1, keepdims=True)
        weights = jnp.exp2(scores - top)
        total = jnp.sum(weights, axis=1, keepdims=True)
        summed = jnp.dot(weights.astype(jnp.bfloat16), values, preferred_element_type=jnp.float32)
        out_ref[:, cols] = (summed / total).astype(out_ref.dtype)
    for copy in own_copies:
        copy.wait()
    own_ref[...] = stream_ref[...].astype(jnp.float32) + jnp.dot(
        hyena_ref[...], weight_ref[...], preferred_element_type=jnp.float32
    )


def shards(
    query_feat,
    key_feat,
    value_feat,
    decay_rate,
    residue,
    conv_skip,
    out_weight,
    stream,
    attn_query,
    attn_key,
    attn_value,
    doc_start,
    read_mask,
):
    rows, channels = query_feat.shape
    order = decay_rate.shape[1]
    state_rows = order * channels // LANES
    f32, bf16 = jnp.float32, jnp.bfloat16
    ctx_count = lax.axis_size("ctx")
    width = out_weight.shape[1] // lax.axis_size("chan")
    core = lax.axis_index("ctx") % 2
    half = state_rows // 2
    state = jax.ShapeDtypeStruct((state_rows, LANES), f32)
    state_half = jax.ShapeDtypeStruct((half, LANES), f32)

    keep, send, rates, block, far_half = pl.pallas_call(
        states_kernel,
        out_shape=(
            state_half,
            state_half,
            state_half,
            jax.ShapeDtypeStruct((2 * rows, attn_key.shape[1]), bf16),
            jax.ShapeDtypeStruct((channels // 2, width), bf16),
        ),
        in_specs=in_hbm(6),
        out_specs=tuple(whole(5)),
        scratch_shapes=[
            VMEM((rows, channels), bf16),
            VMEM((rows, channels), bf16),
            VMEM((order, channels), f32),
            VMEM((8 * rows, LANES), f32),
            VMEM((state_rows, LANES), f32),
            VMEM((state_rows, LANES), f32),
            pltpu.SemaphoreType.DMA((6,)),
        ],
        compiler_params=room(4),
        name="filter_states",
    )(*fixed(key_feat, value_feat, decay_rate.T, attn_key, attn_value, out_weight))
    block_2 = shifted(block, "ctx", 2)
    block_3 = shifted(block_2, "ctx", 1)
    block_1 = core_swap(jnp.where(core == 0, block, block_2))
    far_half = shifted(far_half, "chan", 2)
    far_other = core_swap(far_half)
    got = core_swap(send)
    first = jnp.where(core == 0, keep, got)
    second = jnp.where(core == 0, got, keep)
    both = (first * jnp.exp(-rows * rates) + second).astype(bf16)
    groups = [list(range(c, ctx_count, 2)) for c in range(2)]
    spread = lax.all_to_all(
        jnp.broadcast_to(both, (ctx_count // 2, half, LANES)),
        "ctx",
        0,
        0,
        axis_index_groups=groups,
    )

    columns = jax.ShapeDtypeStruct((channels, width), bf16)
    query, base, steps, scale, *weights = pl.pallas_call(
        local_kernel,
        out_shape=(
            jax.ShapeDtypeStruct((rows, channels), bf16),
            jax.ShapeDtypeStruct((rows, channels), f32),
            state,
            state,
            columns,
            columns,
        ),
        in_specs=whole(1) + in_hbm(7),
        out_specs=tuple(whole(6)),
        scratch_shapes=[
            VMEM((rows, channels), bf16),
            VMEM((rows, channels), bf16),
            VMEM((order, channels), f32),
            VMEM((order, channels), f32),
            VMEM((1, channels), f32),
            VMEM((8 * rows, LANES), f32),
            VMEM((8 * rows, LANES), f32),
            pltpu.SemaphoreType.DMA((14,)),
        ],
        compiler_params=room(6),
        cost_estimate=pl.CostEstimate(flops=0, bytes_accessed=8 * 1024 * 1024, transcendentals=0),
        name="local_part",
    )(
        got,
        *fixed(
            key_feat,
            value_feat,
            decay_rate.T,
            residue.T,
            query_feat,
            conv_skip.reshape(1, channels),
            out_weight,
        ),
    )
    mine, other = pl.pallas_call(
        lambda *refs: carry_kernel(rows, *refs),
        out_shape=(state_half, state_half),
        in_specs=whole(4) + [pl.BlockSpec(memory_space=pl.ANY)],
        out_specs=tuple(whole(2)),
        compiler_params=room(4),
        name="carried_states",
    )(spread, keep, got, rates, steps)
    other = core_swap(other)

    piece = jax.ShapeDtypeStruct((rows, width), bf16)
    hyena = pl.pallas_call(
        gate_kernel,
        out_shape=jax.ShapeDtypeStruct((rows, channels), bf16),
        in_specs=whole(6),
        out_specs=whole(1)[0],
        scratch_shapes=[VMEM((state_rows, LANES), f32), VMEM((8 * rows, LANES), f32)],
        compiler_params=room(4),
        name="gate",
    )(query, base, steps, scale, mine, other)
    near, back = pl.pallas_call(
        near_kernel,
        out_shape=(piece, piece),
        in_specs=whole(3),
        out_specs=tuple(whole(2)),
        compiler_params=room(4),
        name="near",
    )(hyena, *weights)
    far = shifted(hyena, "chan", 2)
    near = shifted(near, "chan", 1)
    back = shifted(back, "chan", 3)

    attended, own, far_weight = pl.pallas_call(
        attention_kernel,
        out_shape=(
            jax.ShapeDtypeStruct(attn_query.shape, bf16),
            jax.ShapeDtypeStruct((rows, width), f32),
            columns,
        ),
        in_specs=in_hbm(9) + whole(2) + [pl.BlockSpec(memory_space=pltpu.SMEM)],
        out_specs=tuple(whole(3)),
        scratch_shapes=[VMEM(attn_query.shape, bf16)]
        + [VMEM((2 * rows, attn_query.shape[1]), bf16)] * 4
        + [
            VMEM((channels, width), bf16),
            VMEM((rows, width), bf16),
            pltpu.SemaphoreType.DMA((4, 5)),
            pltpu.SemaphoreType.DMA((7,)),
        ],
        compiler_params=room(8),
        name="attention",
    )(
        *fixed(attn_query, block, block_1, block_2, block_3),
        *fixed(out_weight, stream, far_half, far_other),
        hyena,
        doc_start.reshape(1, rows),
        read_mask,
    )
    own = pl.pallas_call(
        far_kernel,
        out_shape=jax.ShapeDtypeStruct((rows, width), f32),
        in_specs=whole(3),
        out_specs=whole(1)[0],
        compiler_params=room(4),
        cost_estimate=pl.CostEstimate(flops=0, bytes_accessed=64 << 20, transcendentals=0),
        name="far_product",
    )(own, far, far_weight)
    mixed = pl.pallas_call(
        finish_kernel,
        out_shape=jax.ShapeDtypeStruct(stream.shape, bf16),
        in_specs=whole(3) + [pl.BlockSpec(memory_space=pl.ANY)],
        out_specs=whole(1)[0],
        compiler_params=room(4),
        name="finish",
    )(own, near, back, *fixed(attended))
    return (mixed, attended)


def solution(mesh):
    in_specs = (
        P("ctx", "chan"),
        P("ctx", "chan"),
        P("ctx", "chan"),
        P("chan", None),
        P("chan", None),
        P("chan"),
        P("chan", None),
        P("ctx", "chan"),
        P("ctx", "chan"),
        P("ctx", "chan"),
        P("ctx", "chan"),
        P("ctx"),
        P("ctx", None),
    )
    out_specs = (P("ctx", "chan"), P("ctx", "chan"))
    return jax.shard_map(shards, mesh=mesh, in_specs=in_specs, out_specs=out_specs, check_vma=False)
```

```python
import math

import jax
import jax.numpy as jnp
from jax import lax
from jax.experimental import pallas as pl
from jax.experimental.pallas import tpu as pltpu
from jax.sharding import PartitionSpec as P

HD = 128
LANES = 128
DOC_BLOCKS = 3
VMEM = pltpu.VMEM


def whole(count):
    return [pl.BlockSpec(memory_space=VMEM) for _ in range(count)]


def in_hbm(count):
    return [pl.BlockSpec(memory_space=pltpu.HBM) for _ in range(count)]


def fixed(*values):
    return [pltpu.with_memory_space_constraint(value, pltpu.HBM) for value in values]


def shifted(value, axis, steps):
    count = lax.axis_size(axis)
    return lax.ppermute(value, axis, [(i, (i + steps) % count) for i in range(count)])


def core_swap(value):
    count = lax.axis_size("ctx")
    return lax.ppermute(value, "ctx", [(i, i ^ 1) for i in range(count)])


def room(mib):
    return pltpu.CompilerParams(vmem_limit_bytes=mib * 1024 * 1024)


def to_state_rows(source_ref, target_ref, groups):
    for g in range(groups):
        block = source_ref[:, g * LANES : (g + 1) * LANES]
        target_ref[pl.ds(g, block.shape[0], stride=groups), :] = block


def to_position_rows(product, target_ref, groups):
    rows = product.shape[0]
    for g in range(groups):
        block = product[:, g * LANES : (g + 1) * LANES]
        for half in range(2):
            target_ref[pl.ds(half * groups + g, rows, stride=2 * groups), :] = block


def load(pairs, sems):
    copies = [
        pltpu.make_async_copy(source, target, sems.at[i])
        for i, (source, target) in enumerate(pairs)
    ]
    for copy in copies:
        copy.start()
    return copies


def half_rows(ref, part, half):
    return ref[pl.ds(pl.multiple_of(part * half, half), half), :]


def states_kernel(
    key_hbm,
    value_hbm,
    decay_hbm,
    attn_key_hbm,
    attn_value_hbm,
    weight_hbm,
    keep_ref,
    send_ref,
    rates_ref,
    block_ref,
    far_ref,
    key_ref,
    value_ref,
    decay_ref,
    product_ref,
    all_rates_ref,
    state_ref,
    sems,
):
    core = lax.rem(lax.axis_index("ctx"), 2)
    far_source = weight_columns(weight_hbm, 2, far_ref.shape[1])
    far_rows = pl.ds(pl.multiple_of(core * far_ref.shape[0], far_ref.shape[0]), far_ref.shape[0])
    copies = load(
        [
            (decay_hbm, decay_ref),
            (key_hbm, key_ref),
            (value_hbm, value_ref),
            (far_source.at[far_rows, :], far_ref),
            (attn_key_hbm, block_ref.at[: attn_key_hbm.shape[0]]),
            (attn_value_hbm, block_ref.at[attn_key_hbm.shape[0] :]),
        ],
        sems,
    )
    groups = key_ref.shape[1] // LANES
    rows = key_ref.shape[0]
    copies[0].wait()
    to_state_rows(decay_ref, all_rates_ref, groups)
    count = state_ref.shape[0] // 8
    steps = [jnp.exp(-all_rates_ref[8 * i : 8 * i + 8, :]) for i in range(count)]
    copies[1].wait()
    copies[2].wait()
    product = key_ref[...].astype(jnp.float32) * value_ref[...].astype(jnp.float32)
    to_position_rows(product, product_ref, groups)
    parts = 4
    span = rows // parts
    states = [[jnp.zeros((8, LANES), jnp.float32)] * count for _ in range(parts)]
    for t in range(span):
        for part in range(parts):
            row = 8 * (part * span + t)
            value = product_ref[row : row + 8, :]
            states[part] = [s * a + value for s, a in zip(states[part], steps)]
    for i in range(count):
        long_step = jnp.exp(-span * all_rates_ref[8 * i : 8 * i + 8, :])
        total = states[0][i]
        for part in range(1, parts):
            total = total * long_step + states[part][i]
        state_ref[8 * i : 8 * i + 8, :] = total
    half = keep_ref.shape[0]
    keep_ref[...] = half_rows(state_ref, core, half)
    send_ref[...] = half_rows(state_ref, 1 - core, half)
    rates_ref[...] = half_rows(all_rates_ref, core, half)
    for copy in copies[3:]:
        copy.wait()


def carry_kernel(rows, all_ref, keep_ref, got_ref, rates_ref, *refs):
    mine_ref, other_ref = refs[-2:]
    index = lax.axis_index("ctx")
    core = lax.rem(index, 2)
    chip = lax.div(index, 2)
    half = keep_ref.shape[0]
    rates = rates_ref[...]
    step = jnp.exp(-2 * rows * rates)
    carry = jnp.zeros((half, LANES), jnp.float32)
    for i in range(all_ref.shape[0] - 1):
        carry = jnp.where(i < chip, carry * step + all_ref[i].astype(jnp.float32), carry)
    first = jnp.where(core == 0, keep_ref[...], got_ref[...])
    later = carry * jnp.exp(-rows * rates) + first
    mine_ref[...] = jnp.where(core == 0, carry, later)
    other_ref[...] = jnp.where(core == 0, later, carry)


def local_kernel(
    after_ref,
    key_hbm,
    value_hbm,
    decay_hbm,
    residue_hbm,
    query_hbm,
    skip_hbm,
    weight_hbm,
    query_ref,
    base_ref,
    steps_ref,
    scale_ref,
    near_ref,
    back_ref,
    key_ref,
    value_ref,
    decay_ref,
    residue_ref,
    skip_ref,
    first_ref,
    second_ref,
    product_ref,
    conv_ref,
    sems,
):
    copies = load(
        [
            (decay_hbm, decay_ref),
            (residue_hbm, residue_ref),
            (key_hbm, key_ref),
            (value_hbm, value_ref),
            (query_hbm, query_ref),
            (skip_hbm, skip_ref),
            *weight_pairs(weight_hbm, 1, near_ref),
            *weight_pairs(weight_hbm, 3, back_ref),
        ],
        sems,
    )
    for copy in copies[:-8]:
        copy.wait()
    groups = key_ref.shape[1] // LANES
    rows = key_ref.shape[0]
    state_rows = steps_ref.shape[0]
    to_state_rows(decay_ref, first_ref, groups)
    to_state_rows(residue_ref, second_ref, groups)
    steps_ref[...] = jnp.exp(-first_ref[:state_rows, :])
    scale_ref[...] = second_ref[:state_rows, :]
    product = key_ref[...].astype(jnp.float32) * value_ref[...].astype(jnp.float32)
    to_position_rows(product, product_ref, groups)
    count = steps_ref.shape[0] // 8
    steps = [steps_ref[8 * i : 8 * i + 8, :] for i in range(count)]
    scale = [scale_ref[8 * i : 8 * i + 8, :] for i in range(count)]
    states = [jnp.zeros((8, LANES), jnp.float32)] * count
    for t in range(rows):
        value = product_ref[8 * t : 8 * t + 8, :]
        states = [s * a + value for s, a in zip(states, steps)]
        conv_ref[8 * t : 8 * t + 8, :] = tree_sum([s * w for s, w in zip(states, scale)])
    for g in range(groups):
        lanes = slice(g * LANES, (g + 1) * LANES)
        base_ref[:, lanes] = (
            from_position_rows(conv_ref, g, groups) + skip_ref[:, lanes] * product[:, lanes]
        )
    for copy in copies[-8:]:
        copy.wait()


def tree_sum(terms):
    while len(terms) > 1:
        terms = [u + v for u, v in zip(terms[::2], terms[1::2])]
    return terms[0]


def from_position_rows(source_ref, g, groups):
    rows = source_ref.shape[0] // (2 * groups) - 1
    return (
        source_ref[pl.ds(g, rows, stride=2 * groups), :]
        + source_ref[pl.ds(groups + g, rows, stride=2 * groups), :]
    )


def gate_kernel(
    query_ref,
    base_ref,
    steps_ref,
    scale_ref,
    mine_ref,
    other_ref,
    hyena_ref,
    state_ref,
    conv_ref,
):
    rows = query_ref.shape[0]
    groups = query_ref.shape[1] // LANES
    core = lax.rem(lax.axis_index("ctx"), 2)
    half = mine_ref.shape[0]
    state_ref[pl.ds(pl.multiple_of(core * half, half), half), :] = mine_ref[...]
    state_ref[pl.ds(pl.multiple_of((1 - core) * half, half), half), :] = other_ref[...]
    count = steps_ref.shape[0] // 8
    steps = [steps_ref[8 * i : 8 * i + 8, :] for i in range(count)]
    states = [
        state_ref[8 * i : 8 * i + 8, :] * scale_ref[8 * i : 8 * i + 8, :] for i in range(count)
    ]
    for t in range(rows):
        states = [s * a for s, a in zip(states, steps)]
        conv_ref[8 * t : 8 * t + 8, :] = tree_sum(states)
    for g in range(groups):
        lanes = slice(g * LANES, (g + 1) * LANES)
        conv = from_position_rows(conv_ref, g, groups) + base_ref[:, lanes]
        hyena_ref[:, lanes] = (query_ref[:, lanes].astype(jnp.float32) * conv).astype(
            hyena_ref.dtype
        )


def near_kernel(hyena_ref, near_weight_ref, back_weight_ref, near_ref, back_ref):
    for weight_ref, target in ((near_weight_ref, near_ref), (back_weight_ref, back_ref)):
        target[...] = jnp.dot(
            hyena_ref[...], weight_ref[...], preferred_element_type=jnp.float32
        ).astype(target.dtype)


def weight_pairs(weight_hbm, ahead, target_ref):
    source = weight_columns(weight_hbm, ahead, target_ref.shape[1])
    quarter = target_ref.shape[0] // 4
    rows = [slice(i * quarter, (i + 1) * quarter) for i in range(4)]
    return [(source.at[part, :], target_ref.at[part, :]) for part in rows]


def weight_columns(weight_hbm, ahead, width):
    chan, chans = lax.axis_index("chan"), weight_hbm.shape[1] // width
    column = pl.multiple_of(lax.rem(chan + ahead, chans) * width, width)
    return weight_hbm.at[:, pl.ds(column, width)]


def far_kernel(own_ref, far_ref, weight_ref, out_ref):
    out_ref[...] = own_ref[...] + jnp.dot(
        far_ref[...], weight_ref[...], preferred_element_type=jnp.float32
    )


def finish_kernel(own_ref, near_ref, back_ref, after_ref, out_ref):
    total = own_ref[...] + near_ref[...].astype(jnp.float32) + back_ref[...].astype(jnp.float32)
    out_ref[...] = total.astype(out_ref.dtype)


def attention_kernel(
    query_hbm,
    block_hbm,
    one_hbm,
    two_hbm,
    three_hbm,
    weight_hbm,
    stream_hbm,
    half_hbm,
    other_hbm,
    hyena_ref,
    start_ref,
    read_ref,
    out_ref,
    own_ref,
    far_ref,
    query_ref,
    block_ref,
    one_ref,
    two_ref,
    three_ref,
    weight_ref,
    stream_ref,
    sems,
    own_sems,
):
    core = lax.rem(lax.axis_index("ctx"), 2)
    sources = (query_hbm, block_hbm, one_hbm, two_hbm, three_hbm)
    targets = (query_ref, block_ref, one_ref, two_ref, three_ref)
    chunk = query_ref.shape[1] // 4
    waits = []
    for i in range(4):
        cols = slice(i * chunk, (i + 1) * chunk)
        pairs = [(source.at[:, cols], target.at[:, cols]) for source, target in zip(sources, targets)]
        waits.append(load(pairs, sems.at[i]))
    half = half_hbm.shape[0]
    pairs = [*weight_pairs(weight_hbm, 0, weight_ref), (stream_hbm, stream_ref)]
    for part, source in ((core, half_hbm), (1 - core, other_hbm)):
        part_rows = pl.ds(pl.multiple_of(part * half, half), half)
        pairs.append((source, far_ref.at[part_rows, :]))
    own_copies = load(pairs, own_sems)
    rows = query_ref.shape[0]
    base = lax.axis_index("ctx") * rows
    starts = jnp.broadcast_to(start_ref[...] - base, (rows, rows)).T
    query_pos = lax.broadcasted_iota(jnp.int32, (rows, rows), 0)
    key_pos = lax.broadcasted_iota(jnp.int32, (rows, rows), 1)
    allowed = []
    for back in range(DOC_BLOCKS, -1, -1):
        pos = key_pos - back * rows
        ok = (pos >= starts) & (read_ref[0, back] == 1)
        if back == 0:
            ok = ok & (pos <= query_pos)
        allowed.append(ok)
    mask = jnp.concatenate(allowed, axis=1)
    scale = math.log2(math.e) * HD ** (-0.5)
    blocks = (three_ref, two_ref, one_ref, block_ref)
    for head in range(query_ref.shape[1] // HD):
        if head * HD % chunk == 0:
            for copy in waits[head * HD // chunk]:
                copy.wait()
        cols = slice(head * HD, (head + 1) * HD)
        keys = jnp.concatenate([ref[:rows, cols] for ref in blocks], axis=0)
        values = jnp.concatenate([ref[rows:, cols] for ref in blocks], axis=0)
        scores = lax.dot_general(
            query_ref[:, cols], keys, (((1,), (1,)), ((), ())), preferred_element_type=jnp.float32
        )
        scores = jnp.where(mask, scores * scale, -jnp.inf)
        top = jnp.max(scores, axis=1, keepdims=True)
        weights = jnp.exp2(scores - top)
        total = jnp.sum(weights, axis=1, keepdims=True)
        summed = jnp.dot(weights.astype(jnp.bfloat16), values, preferred_element_type=jnp.float32)
        out_ref[:, cols] = (summed / total).astype(out_ref.dtype)
    for copy in own_copies:
        copy.wait()
    own_ref[...] = stream_ref[...].astype(jnp.float32) + jnp.dot(
        hyena_ref[...], weight_ref[...], preferred_element_type=jnp.float32
    )


def shards(
    query_feat,
    key_feat,
    value_feat,
    decay_rate,
    residue,
    conv_skip,
    out_weight,
    stream,
    attn_query,
    attn_key,
    attn_value,
    doc_start,
    read_mask,
):
    rows, channels = query_feat.shape
    order = decay_rate.shape[1]
    state_rows = order * channels // LANES
    f32, bf16 = jnp.float32, jnp.bfloat16
    ctx_count = lax.axis_size("ctx")
    width = out_weight.shape[1] // lax.axis_size("chan")
    core = lax.axis_index("ctx") % 2
    half = state_rows // 2
    state = jax.ShapeDtypeStruct((state_rows, LANES), f32)
    state_half = jax.ShapeDtypeStruct((half, LANES), f32)

    keep, send, rates, block, far_half = pl.pallas_call(
        states_kernel,
        out_shape=(
            state_half,
            state_half,
            state_half,
            jax.ShapeDtypeStruct((2 * rows, attn_key.shape[1]), bf16),
            jax.ShapeDtypeStruct((channels // 2, width), bf16),
        ),
        in_specs=in_hbm(6),
        out_specs=tuple(whole(5)),
        scratch_shapes=[
            VMEM((rows, channels), bf16),
            VMEM((rows, channels), bf16),
            VMEM((order, channels), f32),
            VMEM((8 * rows + 8, LANES), f32),
            VMEM((state_rows + 8, LANES), f32),
            VMEM((state_rows, LANES), f32),
            pltpu.SemaphoreType.DMA((6,)),
        ],
        compiler_params=room(4),
        name="filter_states",
    )(*fixed(key_feat, value_feat, decay_rate.T, attn_key, attn_value, out_weight))
    block_2 = shifted(block, "ctx", 2)
    block_3 = shifted(block_2, "ctx", 1)
    block_1 = core_swap(jnp.where(core == 0, block, block_2))
    far_half = shifted(far_half, "chan", 2)
    far_other = core_swap(far_half)
    got = core_swap(send)
    first = jnp.where(core == 0, keep, got)
    second = jnp.where(core == 0, got, keep)
    both = (first * jnp.exp(-rows * rates) + second).astype(bf16)
    groups = [list(range(c, ctx_count, 2)) for c in range(2)]
    spread = lax.all_to_all(
        jnp.broadcast_to(both, (ctx_count // 2, half, LANES)),
        "ctx",
        0,
        0,
        axis_index_groups=groups,
    )

    columns = jax.ShapeDtypeStruct((channels, width), bf16)
    query, base, steps, scale, *weights = pl.pallas_call(
        local_kernel,
        out_shape=(
            jax.ShapeDtypeStruct((rows, channels), bf16),
            jax.ShapeDtypeStruct((rows, channels), f32),
            state,
            state,
            columns,
            columns,
        ),
        in_specs=whole(1) + in_hbm(7),
        out_specs=tuple(whole(6)),
        scratch_shapes=[
            VMEM((rows, channels), bf16),
            VMEM((rows, channels), bf16),
            VMEM((order, channels), f32),
            VMEM((order, channels), f32),
            VMEM((1, channels), f32),
            VMEM((state_rows + 8, LANES), f32),
            VMEM((state_rows + 8, LANES), f32),
            VMEM((8 * rows + 8, LANES), f32),
            VMEM((8 * rows + 8, LANES), f32),
            pltpu.SemaphoreType.DMA((14,)),
        ],
        compiler_params=room(6),
        cost_estimate=pl.CostEstimate(flops=0, bytes_accessed=8 * 1024 * 1024, transcendentals=0),
        name="local_part",
    )(
        got,
        *fixed(
            key_feat,
            value_feat,
            decay_rate.T,
            residue.T,
            query_feat,
            conv_skip.reshape(1, channels),
            out_weight,
        ),
    )
    mine, other = pl.pallas_call(
        lambda *refs: carry_kernel(rows, *refs),
        out_shape=(state_half, state_half),
        in_specs=whole(4) + [pl.BlockSpec(memory_space=pl.ANY)],
        out_specs=tuple(whole(2)),
        compiler_params=room(4),
        name="carried_states",
    )(spread, keep, got, rates, steps)
    other = core_swap(other)

    piece = jax.ShapeDtypeStruct((rows, width), bf16)
    hyena = pl.pallas_call(
        gate_kernel,
        out_shape=jax.ShapeDtypeStruct((rows, channels), bf16),
        in_specs=whole(6),
        out_specs=whole(1)[0],
        scratch_shapes=[VMEM((state_rows, LANES), f32), VMEM((8 * rows + 8, LANES), f32)],
        compiler_params=room(4),
        name="gate",
    )(query, base, steps, scale, mine, other)
    near, back = pl.pallas_call(
        near_kernel,
        out_shape=(piece, piece),
        in_specs=whole(3),
        out_specs=tuple(whole(2)),
        compiler_params=room(4),
        name="near",
    )(hyena, *weights)
    far = shifted(hyena, "chan", 2)
    near = shifted(near, "chan", 1)
    back = shifted(back, "chan", 3)

    attended, own, far_weight = pl.pallas_call(
        attention_kernel,
        out_shape=(
            jax.ShapeDtypeStruct(attn_query.shape, bf16),
            jax.ShapeDtypeStruct((rows, width), f32),
            columns,
        ),
        in_specs=in_hbm(9) + whole(2) + [pl.BlockSpec(memory_space=pltpu.SMEM)],
        out_specs=tuple(whole(3)),
        scratch_shapes=[VMEM(attn_query.shape, bf16)]
        + [VMEM((2 * rows, attn_query.shape[1]), bf16)] * 4
        + [
            VMEM((channels, width), bf16),
            VMEM((rows, width), bf16),
            pltpu.SemaphoreType.DMA((4, 5)),
            pltpu.SemaphoreType.DMA((7,)),
        ],
        compiler_params=room(8),
        name="attention",
    )(
        *fixed(attn_query, block, block_1, block_2, block_3),
        *fixed(out_weight, stream, far_half, far_other),
        hyena,
        doc_start.reshape(1, rows),
        read_mask,
    )
    own = pl.pallas_call(
        far_kernel,
        out_shape=jax.ShapeDtypeStruct((rows, width), f32),
        in_specs=whole(3),
        out_specs=whole(1)[0],
        compiler_params=room(4),
        cost_estimate=pl.CostEstimate(flops=0, bytes_accessed=64 << 20, transcendentals=0),
        name="far_product",
    )(own, far, far_weight)
    mixed = pl.pallas_call(
        finish_kernel,
        out_shape=jax.ShapeDtypeStruct(stream.shape, bf16),
        in_specs=whole(3) + [pl.BlockSpec(memory_space=pl.ANY)],
        out_specs=whole(1)[0],
        compiler_params=room(4),
        name="finish",
    )(own, near, back, *fixed(attended))
    return (mixed, attended)


def solution(mesh):
    in_specs = (
        P("ctx", "chan"),
        P("ctx", "chan"),
        P("ctx", "chan"),
        P("chan", None),
        P("chan", None),
        P("chan"),
        P("chan", None),
        P("ctx", "chan"),
        P("ctx", "chan"),
        P("ctx", "chan"),
        P("ctx", "chan"),
        P("ctx"),
        P("ctx", None),
    )
    out_specs = (P("ctx", "chan"), P("ctx", "chan"))
    return jax.shard_map(shards, mesh=mesh, in_specs=in_specs, out_specs=out_specs, check_vma=False)
```

```python
import math

import jax
import jax.numpy as jnp
from jax import lax
from jax.experimental import pallas as pl
from jax.experimental.pallas import tpu as pltpu
from jax.sharding import PartitionSpec as P

HD = 128
LANES = 128
DOC_BLOCKS = 3
VMEM = pltpu.VMEM


def whole(count):
    return [pl.BlockSpec(memory_space=VMEM) for _ in range(count)]


def in_hbm(count):
    return [pl.BlockSpec(memory_space=pltpu.HBM) for _ in range(count)]


def fixed(*values):
    return [pltpu.with_memory_space_constraint(value, pltpu.HBM) for value in values]


def shifted(value, axis, steps):
    count = lax.axis_size(axis)
    return lax.ppermute(value, axis, [(i, (i + steps) % count) for i in range(count)])


def core_swap(value):
    count = lax.axis_size("ctx")
    return lax.ppermute(value, "ctx", [(i, i ^ 1) for i in range(count)])


def room(mib):
    return pltpu.CompilerParams(vmem_limit_bytes=mib * 1024 * 1024)


def to_state_rows(source_ref, target_ref, groups):
    for g in range(groups):
        block = source_ref[:, g * LANES : (g + 1) * LANES]
        target_ref[pl.ds(g, block.shape[0], stride=groups), :] = block


def to_position_rows(product, target_ref, groups):
    rows = product.shape[0]
    for g in range(groups):
        block = product[:, g * LANES : (g + 1) * LANES]
        for half in range(2):
            target_ref[pl.ds(half * groups + g, rows, stride=2 * groups), :] = block


def load(pairs, sems):
    copies = [
        pltpu.make_async_copy(source, target, sems.at[i])
        for i, (source, target) in enumerate(pairs)
    ]
    for copy in copies:
        copy.start()
    return copies


def half_rows(ref, part, half):
    return ref[pl.ds(pl.multiple_of(part * half, half), half), :]


def states_kernel(
    key_hbm,
    value_hbm,
    decay_hbm,
    attn_key_hbm,
    attn_value_hbm,
    weight_hbm,
    keep_ref,
    send_ref,
    rates_ref,
    block_ref,
    far_ref,
    key_ref,
    value_ref,
    decay_ref,
    product_ref,
    all_rates_ref,
    state_ref,
    sems,
):
    core = lax.rem(lax.axis_index("ctx"), 2)
    far_source = weight_columns(weight_hbm, 2, far_ref.shape[1])
    far_rows = pl.ds(pl.multiple_of(core * far_ref.shape[0], far_ref.shape[0]), far_ref.shape[0])
    copies = load(
        [
            (decay_hbm, decay_ref),
            (key_hbm, key_ref),
            (value_hbm, value_ref),
            (far_source.at[far_rows, :], far_ref),
            (attn_key_hbm, block_ref.at[: attn_key_hbm.shape[0]]),
            (attn_value_hbm, block_ref.at[attn_key_hbm.shape[0] :]),
        ],
        sems,
    )
    groups = key_ref.shape[1] // LANES
    rows = key_ref.shape[0]
    copies[0].wait()
    to_state_rows(decay_ref, all_rates_ref, groups)
    count = state_ref.shape[0] // 8
    steps = [jnp.exp(-all_rates_ref[8 * i : 8 * i + 8, :]) for i in range(count)]
    copies[1].wait()
    copies[2].wait()
    product = key_ref[...].astype(jnp.float32) * value_ref[...].astype(jnp.float32)
    to_position_rows(product, product_ref, groups)
    parts = 4
    span = rows // parts
    states = [[jnp.zeros((8, LANES), jnp.float32)] * count for _ in range(parts)]
    for t in range(span):
        for part in range(parts):
            row = 8 * (part * span + t)
            value = product_ref[row : row + 8, :]
            states[part] = [s * a + value for s, a in zip(states[part], steps)]
    for i in range(count):
        long_step = jnp.exp(-span * all_rates_ref[8 * i : 8 * i + 8, :])
        total = states[0][i]
        for part in range(1, parts):
            total = total * long_step + states[part][i]
        state_ref[8 * i : 8 * i + 8, :] = total
    half = keep_ref.shape[0]
    keep_ref[...] = half_rows(state_ref, core, half)
    send_ref[...] = half_rows(state_ref, 1 - core, half)
    rates_ref[...] = half_rows(all_rates_ref, core, half)
    for copy in copies[3:]:
        copy.wait()


def carry_kernel(rows, all_ref, keep_ref, got_ref, rates_ref, *refs):
    mine_ref, other_ref = refs[-2:]
    index = lax.axis_index("ctx")
    core = lax.rem(index, 2)
    chip = lax.div(index, 2)
    half = keep_ref.shape[0]
    rates = rates_ref[...]
    step = jnp.exp(-2 * rows * rates)
    carry = jnp.zeros((half, LANES), jnp.float32)
    for i in range(all_ref.shape[0] - 1):
        carry = jnp.where(i < chip, carry * step + all_ref[i].astype(jnp.float32), carry)
    first = jnp.where(core == 0, keep_ref[...], got_ref[...])
    later = carry * jnp.exp(-rows * rates) + first
    mine_ref[...] = jnp.where(core == 0, carry, later)
    other_ref[...] = jnp.where(core == 0, later, carry)


def local_kernel(
    after_ref,
    key_hbm,
    value_hbm,
    decay_hbm,
    residue_hbm,
    query_hbm,
    skip_hbm,
    weight_hbm,
    query_ref,
    base_ref,
    steps_ref,
    scale_ref,
    near_ref,
    back_ref,
    key_ref,
    value_ref,
    decay_ref,
    residue_ref,
    skip_ref,
    first_ref,
    second_ref,
    product_ref,
    conv_ref,
    sems,
):
    copies = load(
        [
            (decay_hbm, decay_ref),
            (residue_hbm, residue_ref),
            (key_hbm, key_ref),
            (value_hbm, value_ref),
            (query_hbm, query_ref),
            (skip_hbm, skip_ref),
            *weight_pairs(weight_hbm, 1, near_ref),
            *weight_pairs(weight_hbm, 3, back_ref),
        ],
        sems,
    )
    for copy in copies[:-8]:
        copy.wait()
    groups = key_ref.shape[1] // LANES
    rows = key_ref.shape[0]
    state_rows = steps_ref.shape[0]
    to_state_rows(decay_ref, first_ref, groups)
    to_state_rows(residue_ref, second_ref, groups)
    steps_ref[...] = jnp.exp(-first_ref[:state_rows, :])
    scale_ref[...] = second_ref[:state_rows, :]
    product = key_ref[...].astype(jnp.float32) * value_ref[...].astype(jnp.float32)
    to_position_rows(product, product_ref, groups)
    count = steps_ref.shape[0] // 8
    steps = [steps_ref[8 * i : 8 * i + 8, :] for i in range(count)]
    scale = [scale_ref[8 * i : 8 * i + 8, :] for i in range(count)]
    states = [jnp.zeros((8, LANES), jnp.float32)] * count
    for t in range(rows):
        value = product_ref[8 * t : 8 * t + 8, :]
        states = [s * a + value for s, a in zip(states, steps)]
        conv_ref[8 * t : 8 * t + 8, :] = tree_sum([s * w for s, w in zip(states, scale)])
    for g in range(groups):
        lanes = slice(g * LANES, (g + 1) * LANES)
        base_ref[:, lanes] = (
            from_position_rows(conv_ref, g, groups) + skip_ref[:, lanes] * product[:, lanes]
        )
    for copy in copies[-8:]:
        copy.wait()


def tree_sum(terms):
    while len(terms) > 1:
        terms = [u + v for u, v in zip(terms[::2], terms[1::2])]
    return terms[0]


def from_position_rows(source_ref, g, groups):
    rows = source_ref.shape[0] // (2 * groups) - 1
    return (
        source_ref[pl.ds(g, rows, stride=2 * groups), :]
        + source_ref[pl.ds(groups + g, rows, stride=2 * groups), :]
    )


def gate_kernel(
    query_ref,
    base_ref,
    steps_ref,
    scale_ref,
    mine_ref,
    other_ref,
    near_weight_ref,
    back_weight_ref,
    hyena_ref,
    near_ref,
    back_ref,
    state_ref,
    conv_ref,
):
    rows = query_ref.shape[0]
    groups = query_ref.shape[1] // LANES
    core = lax.rem(lax.axis_index("ctx"), 2)
    half = mine_ref.shape[0]
    state_ref[pl.ds(pl.multiple_of(core * half, half), half), :] = mine_ref[...]
    state_ref[pl.ds(pl.multiple_of((1 - core) * half, half), half), :] = other_ref[...]
    count = steps_ref.shape[0] // 8
    steps = [steps_ref[8 * i : 8 * i + 8, :] for i in range(count)]
    states = [
        state_ref[8 * i : 8 * i + 8, :] * scale_ref[8 * i : 8 * i + 8, :] for i in range(count)
    ]
    for t in range(rows):
        states = [s * a for s, a in zip(states, steps)]
        conv_ref[8 * t : 8 * t + 8, :] = tree_sum(states)
    for g in range(groups):
        lanes = slice(g * LANES, (g + 1) * LANES)
        conv = from_position_rows(conv_ref, g, groups) + base_ref[:, lanes]
        hyena_ref[:, lanes] = (query_ref[:, lanes].astype(jnp.float32) * conv).astype(
            hyena_ref.dtype
        )
    for weight_ref, target in ((near_weight_ref, near_ref), (back_weight_ref, back_ref)):
        target[...] = jnp.dot(
            hyena_ref[...], weight_ref[...], preferred_element_type=jnp.float32
        ).astype(target.dtype)


def weight_pairs(weight_hbm, ahead, target_ref):
    source = weight_columns(weight_hbm, ahead, target_ref.shape[1])
    quarter = target_ref.shape[0] // 4
    rows = [slice(i * quarter, (i + 1) * quarter) for i in range(4)]
    return [(source.at[part, :], target_ref.at[part, :]) for part in rows]


def weight_columns(weight_hbm, ahead, width):
    chan, chans = lax.axis_index("chan"), weight_hbm.shape[1] // width
    column = pl.multiple_of(lax.rem(chan + ahead, chans) * width, width)
    return weight_hbm.at[:, pl.ds(column, width)]


def finish_kernel(
    own_ref, near_ref, back_ref, far_ref, weight_ref, after_ref, out_hbm, out_ref, sems
):
    pieces = sems.shape[0]
    width = out_ref.shape[1] // pieces
    copies = []
    for i in range(pieces):
        lanes = slice(i * width, (i + 1) * width)
        total = own_ref[:, lanes] + near_ref[:, lanes].astype(jnp.float32)
        total = total + back_ref[:, lanes].astype(jnp.float32)
        total = total + jnp.dot(
            far_ref[...], weight_ref[:, lanes], preferred_element_type=jnp.float32
        )
        out_ref[:, lanes] = total.astype(out_ref.dtype)
        copy = pltpu.make_async_copy(out_ref.at[:, lanes], out_hbm.at[:, lanes], sems.at[i])
        copy.start()
        copies.append(copy)
    for copy in copies:
        copy.wait()


def attention_kernel(
    query_hbm,
    block_hbm,
    one_hbm,
    two_hbm,
    three_hbm,
    weight_hbm,
    stream_hbm,
    half_hbm,
    other_hbm,
    hyena_ref,
    start_ref,
    read_ref,
    out_ref,
    own_ref,
    far_ref,
    query_ref,
    block_ref,
    one_ref,
    two_ref,
    three_ref,
    weight_ref,
    stream_ref,
    sems,
    own_sems,
):
    core = lax.rem(lax.axis_index("ctx"), 2)
    sources = (query_hbm, block_hbm, one_hbm, two_hbm, three_hbm)
    targets = (query_ref, block_ref, one_ref, two_ref, three_ref)
    chunk = query_ref.shape[1] // 4
    waits = []
    for i in range(4):
        cols = slice(i * chunk, (i + 1) * chunk)
        pairs = [(source.at[:, cols], target.at[:, cols]) for source, target in zip(sources, targets)]
        waits.append(load(pairs, sems.at[i]))
    half = half_hbm.shape[0]
    pairs = [*weight_pairs(weight_hbm, 0, weight_ref), (stream_hbm, stream_ref)]
    for part, source in ((core, half_hbm), (1 - core, other_hbm)):
        part_rows = pl.ds(pl.multiple_of(part * half, half), half)
        pairs.append((source, far_ref.at[part_rows, :]))
    own_copies = load(pairs, own_sems)
    rows = query_ref.shape[0]
    base = lax.axis_index("ctx") * rows
    starts = jnp.broadcast_to(start_ref[...] - base, (rows, rows)).T
    query_pos = lax.broadcasted_iota(jnp.int32, (rows, rows), 0)
    key_pos = lax.broadcasted_iota(jnp.int32, (rows, rows), 1)
    allowed = []
    for back in range(DOC_BLOCKS, -1, -1):
        pos = key_pos - back * rows
        ok = (pos >= starts) & (read_ref[0, back] == 1)
        if back == 0:
            ok = ok & (pos <= query_pos)
        allowed.append(ok)
    mask = jnp.concatenate(allowed, axis=1)
    scale = math.log2(math.e) * HD ** (-0.5)
    blocks = (three_ref, two_ref, one_ref, block_ref)
    for head in range(query_ref.shape[1] // HD):
        if head * HD % chunk == 0:
            for copy in waits[head * HD // chunk]:
                copy.wait()
        cols = slice(head * HD, (head + 1) * HD)
        keys = jnp.concatenate([ref[:rows, cols] for ref in blocks], axis=0)
        values = jnp.concatenate([ref[rows:, cols] for ref in blocks], axis=0)
        scores = lax.dot_general(
            query_ref[:, cols], keys, (((1,), (1,)), ((), ())), preferred_element_type=jnp.float32
        )
        scores = jnp.where(mask, scores * scale, -jnp.inf)
        top = jnp.max(scores, axis=1, keepdims=True)
        weights = jnp.exp2(scores - top)
        total = jnp.sum(weights, axis=1, keepdims=True)
        summed = jnp.dot(weights.astype(jnp.bfloat16), values, preferred_element_type=jnp.float32)
        out_ref[:, cols] = (summed / total).astype(out_ref.dtype)
    for copy in own_copies:
        copy.wait()
    own_ref[...] = stream_ref[...].astype(jnp.float32) + jnp.dot(
        hyena_ref[...], weight_ref[...], preferred_element_type=jnp.float32
    )


def shards(
    query_feat,
    key_feat,
    value_feat,
    decay_rate,
    residue,
    conv_skip,
    out_weight,
    stream,
    attn_query,
    attn_key,
    attn_value,
    doc_start,
    read_mask,
):
    rows, channels = query_feat.shape
    order = decay_rate.shape[1]
    state_rows = order * channels // LANES
    f32, bf16 = jnp.float32, jnp.bfloat16
    ctx_count = lax.axis_size("ctx")
    width = out_weight.shape[1] // lax.axis_size("chan")
    core = lax.axis_index("ctx") % 2
    half = state_rows // 2
    state = jax.ShapeDtypeStruct((state_rows, LANES), f32)
    state_half = jax.ShapeDtypeStruct((half, LANES), f32)

    keep, send, rates, block, far_half = pl.pallas_call(
        states_kernel,
        out_shape=(
            state_half,
            state_half,
            state_half,
            jax.ShapeDtypeStruct((2 * rows, attn_key.shape[1]), bf16),
            jax.ShapeDtypeStruct((channels // 2, width), bf16),
        ),
        in_specs=in_hbm(6),
        out_specs=tuple(whole(5)),
        scratch_shapes=[
            VMEM((rows, channels), bf16),
            VMEM((rows, channels), bf16),
            VMEM((order, channels), f32),
            VMEM((8 * rows + 8, LANES), f32),
            VMEM((state_rows + 8, LANES), f32),
            VMEM((state_rows, LANES), f32),
            pltpu.SemaphoreType.DMA((6,)),
        ],
        compiler_params=room(4),
        name="filter_states",
    )(*fixed(key_feat, value_feat, decay_rate.T, attn_key, attn_value, out_weight))
    block_2 = shifted(block, "ctx", 2)
    block_3 = shifted(block_2, "ctx", 1)
    block_1 = core_swap(jnp.where(core == 0, block, block_2))
    far_half = shifted(far_half, "chan", 2)
    far_other = core_swap(far_half)
    got = core_swap(send)
    first = jnp.where(core == 0, keep, got)
    second = jnp.where(core == 0, got, keep)
    both = (first * jnp.exp(-rows * rates) + second).astype(bf16)
    groups = [list(range(c, ctx_count, 2)) for c in range(2)]
    spread = lax.all_to_all(
        jnp.broadcast_to(both, (ctx_count // 2, half, LANES)),
        "ctx",
        0,
        0,
        axis_index_groups=groups,
    )

    columns = jax.ShapeDtypeStruct((channels, width), bf16)
    query, base, steps, scale, *weights = pl.pallas_call(
        local_kernel,
        out_shape=(
            jax.ShapeDtypeStruct((rows, channels), bf16),
            jax.ShapeDtypeStruct((rows, channels), f32),
            state,
            state,
            columns,
            columns,
        ),
        in_specs=whole(1) + in_hbm(7),
        out_specs=tuple(whole(6)),
        scratch_shapes=[
            VMEM((rows, channels), bf16),
            VMEM((rows, channels), bf16),
            VMEM((order, channels), f32),
            VMEM((order, channels), f32),
            VMEM((1, channels), f32),
            VMEM((state_rows + 8, LANES), f32),
            VMEM((state_rows + 8, LANES), f32),
            VMEM((8 * rows + 8, LANES), f32),
            VMEM((8 * rows + 8, LANES), f32),
            pltpu.SemaphoreType.DMA((14,)),
        ],
        compiler_params=room(6),
        cost_estimate=pl.CostEstimate(flops=0, bytes_accessed=8 * 1024 * 1024, transcendentals=0),
        name="local_part",
    )(
        got,
        *fixed(
            key_feat,
            value_feat,
            decay_rate.T,
            residue.T,
            query_feat,
            conv_skip.reshape(1, channels),
            out_weight,
        ),
    )
    mine, other = pl.pallas_call(
        lambda *refs: carry_kernel(rows, *refs),
        out_shape=(state_half, state_half),
        in_specs=whole(4) + [pl.BlockSpec(memory_space=pl.ANY)],
        out_specs=tuple(whole(2)),
        compiler_params=room(4),
        name="carried_states",
    )(spread, keep, got, rates, steps)
    other = core_swap(other)

    piece = jax.ShapeDtypeStruct((rows, width), bf16)
    hyena, near, back = pl.pallas_call(
        gate_kernel,
        out_shape=(jax.ShapeDtypeStruct((rows, channels), bf16), piece, piece),
        in_specs=whole(8),
        out_specs=tuple(whole(3)),
        scratch_shapes=[VMEM((state_rows, LANES), f32), VMEM((8 * rows + 8, LANES), f32)],
        compiler_params=room(4),
        name="gate",
    )(query, base, steps, scale, mine, other, *weights)
    far = shifted(hyena, "chan", 2)
    near = shifted(near, "chan", 1)
    back = shifted(back, "chan", 3)

    attended, own, far_weight = pl.pallas_call(
        attention_kernel,
        out_shape=(
            jax.ShapeDtypeStruct(attn_query.shape, bf16),
            jax.ShapeDtypeStruct((rows, width), f32),
            columns,
        ),
        in_specs=in_hbm(9) + whole(2) + [pl.BlockSpec(memory_space=pltpu.SMEM)],
        out_specs=tuple(whole(3)),
        scratch_shapes=[VMEM(attn_query.shape, bf16)]
        + [VMEM((2 * rows, attn_query.shape[1]), bf16)] * 4
        + [
            VMEM((channels, width), bf16),
            VMEM((rows, width), bf16),
            pltpu.SemaphoreType.DMA((4, 5)),
            pltpu.SemaphoreType.DMA((7,)),
        ],
        compiler_params=room(8),
        name="attention",
    )(
        *fixed(attn_query, block, block_1, block_2, block_3),
        *fixed(out_weight, stream, far_half, far_other),
        hyena,
        doc_start.reshape(1, rows),
        read_mask,
    )
    mixed = pl.pallas_call(
        finish_kernel,
        out_shape=jax.ShapeDtypeStruct(stream.shape, bf16),
        in_specs=whole(5) + [pl.BlockSpec(memory_space=pl.ANY)],
        out_specs=in_hbm(1)[0],
        scratch_shapes=[VMEM(stream.shape, bf16), pltpu.SemaphoreType.DMA((4,))],
        compiler_params=room(4),
        name="finish",
    )(own, near, back, far, far_weight, *fixed(attended))
    return (mixed, attended)


def solution(mesh):
    in_specs = (
        P("ctx", "chan"),
        P("ctx", "chan"),
        P("ctx", "chan"),
        P("chan", None),
        P("chan", None),
        P("chan"),
        P("chan", None),
        P("ctx", "chan"),
        P("ctx", "chan"),
        P("ctx", "chan"),
        P("ctx", "chan"),
        P("ctx"),
        P("ctx", None),
    )
    out_specs = (P("ctx", "chan"), P("ctx", "chan"))
    return jax.shard_map(shards, mesh=mesh, in_specs=in_specs, out_specs=out_specs, check_vma=False)
```

```python
import math

import jax
import jax.numpy as jnp
from jax import lax
from jax.experimental import pallas as pl
from jax.experimental.pallas import tpu as pltpu
from jax.sharding import PartitionSpec as P

HD = 128
LANES = 128
DOC_BLOCKS = 3
VMEM = pltpu.VMEM


def whole(count):
    return [pl.BlockSpec(memory_space=VMEM) for _ in range(count)]


def in_hbm(count):
    return [pl.BlockSpec(memory_space=pltpu.HBM) for _ in range(count)]


def fixed(*values):
    return [pltpu.with_memory_space_constraint(value, pltpu.HBM) for value in values]


def shifted(value, axis, steps):
    count = lax.axis_size(axis)
    return lax.ppermute(value, axis, [(i, (i + steps) % count) for i in range(count)])


def core_swap(value):
    count = lax.axis_size("ctx")
    return lax.ppermute(value, "ctx", [(i, i ^ 1) for i in range(count)])


def room(mib):
    return pltpu.CompilerParams(vmem_limit_bytes=mib * 1024 * 1024)


def to_state_rows(source_ref, target_ref, groups):
    for g in range(groups):
        block = source_ref[:, g * LANES : (g + 1) * LANES]
        target_ref[pl.ds(g, block.shape[0], stride=groups), :] = block


def to_position_rows(product, target_ref, groups):
    rows = product.shape[0]
    for g in range(groups):
        block = product[:, g * LANES : (g + 1) * LANES]
        for half in range(2):
            target_ref[pl.ds(half * groups + g, rows, stride=2 * groups), :] = block


def load(pairs, sems):
    copies = [
        pltpu.make_async_copy(source, target, sems.at[i])
        for i, (source, target) in enumerate(pairs)
    ]
    for copy in copies:
        copy.start()
    return copies


def half_rows(ref, part, half):
    return ref[pl.ds(pl.multiple_of(part * half, half), half), :]


def states_kernel(
    key_hbm,
    value_hbm,
    decay_hbm,
    attn_key_hbm,
    attn_value_hbm,
    weight_hbm,
    keep_ref,
    send_ref,
    rates_ref,
    block_ref,
    far_ref,
    key_ref,
    value_ref,
    decay_ref,
    product_ref,
    all_rates_ref,
    state_ref,
    sems,
):
    core = lax.rem(lax.axis_index("ctx"), 2)
    far_source = weight_columns(weight_hbm, 2, far_ref.shape[1])
    far_rows = pl.ds(pl.multiple_of(core * far_ref.shape[0], far_ref.shape[0]), far_ref.shape[0])
    copies = load(
        [
            (decay_hbm, decay_ref),
            (key_hbm, key_ref),
            (value_hbm, value_ref),
            (far_source.at[far_rows, :], far_ref),
            (attn_key_hbm, block_ref.at[: attn_key_hbm.shape[0]]),
            (attn_value_hbm, block_ref.at[attn_key_hbm.shape[0] :]),
        ],
        sems,
    )
    groups = key_ref.shape[1] // LANES
    rows = key_ref.shape[0]
    copies[0].wait()
    to_state_rows(decay_ref, all_rates_ref, groups)
    count = state_ref.shape[0] // 8
    steps = [jnp.exp(-all_rates_ref[8 * i : 8 * i + 8, :]) for i in range(count)]
    copies[1].wait()
    copies[2].wait()
    product = key_ref[...].astype(jnp.float32) * value_ref[...].astype(jnp.float32)
    to_position_rows(product, product_ref, groups)
    parts = 4
    span = rows // parts
    states = [[jnp.zeros((8, LANES), jnp.float32)] * count for _ in range(parts)]
    for t in range(span):
        for part in range(parts):
            row = 8 * (part * span + t)
            value = product_ref[row : row + 8, :]
            states[part] = [s * a + value for s, a in zip(states[part], steps)]
    for i in range(count):
        long_step = jnp.exp(-span * all_rates_ref[8 * i : 8 * i + 8, :])
        total = states[0][i]
        for part in range(1, parts):
            total = total * long_step + states[part][i]
        state_ref[8 * i : 8 * i + 8, :] = total
    half = keep_ref.shape[0]
    keep_ref[...] = half_rows(state_ref, core, half)
    for i in range(send_ref.shape[0]):
        send_ref[i] = half_rows(state_ref, 1 - core, half)
    rates_ref[...] = half_rows(all_rates_ref, core, half)
    for copy in copies[3:]:
        copy.wait()


def carry_kernel(rows, all_ref, keep_ref, got_ref, rates_ref, *refs):
    mine_ref, other_ref = refs[-2:]
    index = lax.axis_index("ctx")
    core = lax.rem(index, 2)
    chip = lax.div(index, 2)
    half = keep_ref.shape[0]
    rates = rates_ref[...]
    step = jnp.exp(-2 * rows * rates)
    carry = jnp.zeros((half, LANES), jnp.float32)
    for i in range(all_ref.shape[0] - 1):
        carry = jnp.where(i < chip, carry * step + all_ref[i].astype(jnp.float32), carry)
    first = jnp.where(core == 0, keep_ref[...], got_ref[...])
    later = carry * jnp.exp(-rows * rates) + first
    mine_ref[...] = jnp.where(core == 0, carry, later)
    other_ref[...] = jnp.where(core == 0, later, carry)


def local_kernel(
    after_ref,
    key_hbm,
    value_hbm,
    decay_hbm,
    residue_hbm,
    query_hbm,
    skip_hbm,
    weight_hbm,
    query_ref,
    base_ref,
    steps_ref,
    scale_ref,
    near_ref,
    back_ref,
    key_ref,
    value_ref,
    decay_ref,
    residue_ref,
    skip_ref,
    first_ref,
    second_ref,
    product_ref,
    conv_ref,
    sems,
):
    copies = load(
        [
            (decay_hbm, decay_ref),
            (residue_hbm, residue_ref),
            (key_hbm, key_ref),
            (value_hbm, value_ref),
            (query_hbm, query_ref),
            (skip_hbm, skip_ref),
            *weight_pairs(weight_hbm, 1, near_ref),
            *weight_pairs(weight_hbm, 3, back_ref),
        ],
        sems,
    )
    for copy in copies[:-8]:
        copy.wait()
    groups = key_ref.shape[1] // LANES
    rows = key_ref.shape[0]
    state_rows = steps_ref.shape[0]
    to_state_rows(decay_ref, first_ref, groups)
    to_state_rows(residue_ref, second_ref, groups)
    steps_ref[...] = jnp.exp(-first_ref[:state_rows, :])
    scale_ref[...] = second_ref[:state_rows, :]
    product = key_ref[...].astype(jnp.float32) * value_ref[...].astype(jnp.float32)
    to_position_rows(product, product_ref, groups)
    count = steps_ref.shape[0] // 8
    steps = [steps_ref[8 * i : 8 * i + 8, :] for i in range(count)]
    scale = [scale_ref[8 * i : 8 * i + 8, :] for i in range(count)]
    states = [jnp.zeros((8, LANES), jnp.float32)] * count
    for t in range(rows):
        value = product_ref[8 * t : 8 * t + 8, :]
        states = [s * a + value for s, a in zip(states, steps)]
        conv_ref[8 * t : 8 * t + 8, :] = tree_sum([s * w for s, w in zip(states, scale)])
    for g in range(groups):
        lanes = slice(g * LANES, (g + 1) * LANES)
        base_ref[:, lanes] = (
            from_position_rows(conv_ref, g, groups) + skip_ref[:, lanes] * product[:, lanes]
        )
    for copy in copies[-8:]:
        copy.wait()


def tree_sum(terms):
    while len(terms) > 1:
        terms = [u + v for u, v in zip(terms[::2], terms[1::2])]
    return terms[0]


def from_position_rows(source_ref, g, groups):
    rows = source_ref.shape[0] // (2 * groups) - 1
    return (
        source_ref[pl.ds(g, rows, stride=2 * groups), :]
        + source_ref[pl.ds(groups + g, rows, stride=2 * groups), :]
    )


def gate_kernel(
    query_ref,
    base_ref,
    steps_ref,
    scale_ref,
    mine_ref,
    other_ref,
    near_weight_ref,
    back_weight_ref,
    hyena_ref,
    near_ref,
    back_ref,
    state_ref,
    conv_ref,
):
    rows = query_ref.shape[0]
    groups = query_ref.shape[1] // LANES
    core = lax.rem(lax.axis_index("ctx"), 2)
    half = mine_ref.shape[0]
    state_ref[pl.ds(pl.multiple_of(core * half, half), half), :] = mine_ref[...]
    state_ref[pl.ds(pl.multiple_of((1 - core) * half, half), half), :] = other_ref[...]
    count = steps_ref.shape[0] // 8
    steps = [steps_ref[8 * i : 8 * i + 8, :] for i in range(count)]
    states = [
        state_ref[8 * i : 8 * i + 8, :] * scale_ref[8 * i : 8 * i + 8, :] for i in range(count)
    ]
    for t in range(rows):
        states = [s * a for s, a in zip(states, steps)]
        conv_ref[8 * t : 8 * t + 8, :] = tree_sum(states)
    for g in range(groups):
        lanes = slice(g * LANES, (g + 1) * LANES)
        conv = from_position_rows(conv_ref, g, groups) + base_ref[:, lanes]
        hyena_ref[:, lanes] = (query_ref[:, lanes].astype(jnp.float32) * conv).astype(
            hyena_ref.dtype
        )
    for weight_ref, target in ((near_weight_ref, near_ref), (back_weight_ref, back_ref)):
        target[...] = jnp.dot(
            hyena_ref[...], weight_ref[...], preferred_element_type=jnp.float32
        ).astype(target.dtype)


def weight_pairs(weight_hbm, ahead, target_ref):
    source = weight_columns(weight_hbm, ahead, target_ref.shape[1])
    quarter = target_ref.shape[0] // 4
    rows = [slice(i * quarter, (i + 1) * quarter) for i in range(4)]
    return [(source.at[part, :], target_ref.at[part, :]) for part in rows]


def weight_columns(weight_hbm, ahead, width):
    chan, chans = lax.axis_index("chan"), weight_hbm.shape[1] // width
    column = pl.multiple_of(lax.rem(chan + ahead, chans) * width, width)
    return weight_hbm.at[:, pl.ds(column, width)]


def finish_kernel(
    own_ref, near_ref, back_ref, far_ref, weight_ref, after_ref, out_hbm, out_ref, sems
):
    pieces = sems.shape[0]
    width = out_ref.shape[1] // pieces
    copies = []
    for i in range(pieces):
        lanes = slice(i * width, (i + 1) * width)
        total = own_ref[:, lanes] + near_ref[:, lanes].astype(jnp.float32)
        total = total + back_ref[:, lanes].astype(jnp.float32)
        total = total + jnp.dot(
            far_ref[...], weight_ref[:, lanes], preferred_element_type=jnp.float32
        )
        out_ref[:, lanes] = total.astype(out_ref.dtype)
        copy = pltpu.make_async_copy(out_ref.at[:, lanes], out_hbm.at[:, lanes], sems.at[i])
        copy.start()
        copies.append(copy)
    for copy in copies:
        copy.wait()


def attention_kernel(
    query_hbm,
    block_hbm,
    one_hbm,
    two_hbm,
    three_hbm,
    weight_hbm,
    stream_hbm,
    half_hbm,
    other_hbm,
    hyena_ref,
    start_ref,
    read_ref,
    out_ref,
    own_ref,
    far_ref,
    query_ref,
    block_ref,
    one_ref,
    two_ref,
    three_ref,
    weight_ref,
    stream_ref,
    sems,
    own_sems,
):
    core = lax.rem(lax.axis_index("ctx"), 2)
    sources = (query_hbm, block_hbm, one_hbm, two_hbm, three_hbm)
    targets = (query_ref, block_ref, one_ref, two_ref, three_ref)
    chunk = query_ref.shape[1] // 4
    waits = []
    for i in range(4):
        cols = slice(i * chunk, (i + 1) * chunk)
        pairs = [(source.at[:, cols], target.at[:, cols]) for source, target in zip(sources, targets)]
        waits.append(load(pairs, sems.at[i]))
    half = half_hbm.shape[0]
    pairs = [*weight_pairs(weight_hbm, 0, weight_ref), (stream_hbm, stream_ref)]
    for part, source in ((core, half_hbm), (1 - core, other_hbm)):
        part_rows = pl.ds(pl.multiple_of(part * half, half), half)
        pairs.append((source, far_ref.at[part_rows, :]))
    own_copies = load(pairs, own_sems)
    rows = query_ref.shape[0]
    base = lax.axis_index("ctx") * rows
    starts = jnp.broadcast_to(start_ref[...] - base, (rows, rows)).T
    query_pos = lax.broadcasted_iota(jnp.int32, (rows, rows), 0)
    key_pos = lax.broadcasted_iota(jnp.int32, (rows, rows), 1)
    allowed = []
    for back in range(DOC_BLOCKS, -1, -1):
        pos = key_pos - back * rows
        ok = (pos >= starts) & (read_ref[0, back] == 1)
        if back == 0:
            ok = ok & (pos <= query_pos)
        allowed.append(ok)
    mask = jnp.concatenate(allowed, axis=1)
    scale = math.log2(math.e) * HD ** (-0.5)
    blocks = (three_ref, two_ref, one_ref, block_ref)
    for head in range(query_ref.shape[1] // HD):
        if head * HD % chunk == 0:
            for copy in waits[head * HD // chunk]:
                copy.wait()
        cols = slice(head * HD, (head + 1) * HD)
        keys = jnp.concatenate([ref[:rows, cols] for ref in blocks], axis=0)
        values = jnp.concatenate([ref[rows:, cols] for ref in blocks], axis=0)
        scores = lax.dot_general(
            query_ref[:, cols], keys, (((1,), (1,)), ((), ())), preferred_element_type=jnp.float32
        )
        scores = jnp.where(mask, scores * scale, -jnp.inf)
        top = jnp.max(scores, axis=1, keepdims=True)
        weights = jnp.exp2(scores - top)
        total = jnp.sum(weights, axis=1, keepdims=True)
        summed = jnp.dot(weights.astype(jnp.bfloat16), values, preferred_element_type=jnp.float32)
        out_ref[:, cols] = (summed / total).astype(out_ref.dtype)
    for copy in own_copies:
        copy.wait()
    own_ref[...] = stream_ref[...].astype(jnp.float32) + jnp.dot(
        hyena_ref[...], weight_ref[...], preferred_element_type=jnp.float32
    )


def shards(
    query_feat,
    key_feat,
    value_feat,
    decay_rate,
    residue,
    conv_skip,
    out_weight,
    stream,
    attn_query,
    attn_key,
    attn_value,
    doc_start,
    read_mask,
):
    rows, channels = query_feat.shape
    order = decay_rate.shape[1]
    state_rows = order * channels // LANES
    f32, bf16 = jnp.float32, jnp.bfloat16
    ctx_count = lax.axis_size("ctx")
    width = out_weight.shape[1] // lax.axis_size("chan")
    core = lax.axis_index("ctx") % 2
    half = state_rows // 2
    state = jax.ShapeDtypeStruct((state_rows, LANES), f32)
    state_half = jax.ShapeDtypeStruct((half, LANES), f32)

    keep, send, rates, block, far_half = pl.pallas_call(
        states_kernel,
        out_shape=(
            state_half,
            jax.ShapeDtypeStruct((20, half, LANES), f32),
            state_half,
            jax.ShapeDtypeStruct((2 * rows, attn_key.shape[1]), bf16),
            jax.ShapeDtypeStruct((channels // 2, width), bf16),
        ),
        in_specs=in_hbm(6),
        out_specs=tuple(whole(5)),
        scratch_shapes=[
            VMEM((rows, channels), bf16),
            VMEM((rows, channels), bf16),
            VMEM((order, channels), f32),
            VMEM((8 * rows + 8, LANES), f32),
            VMEM((state_rows + 8, LANES), f32),
            VMEM((state_rows, LANES), f32),
            pltpu.SemaphoreType.DMA((6,)),
        ],
        compiler_params=room(4),
        name="filter_states",
    )(*fixed(key_feat, value_feat, decay_rate.T, attn_key, attn_value, out_weight))
    block_2 = shifted(block, "ctx", 2)
    block_3 = shifted(block_2, "ctx", 1)
    block_1 = core_swap(jnp.where(core == 0, block, block_2))
    far_half = shifted(far_half, "chan", 2)
    far_other = core_swap(far_half)
    got = core_swap(send)[0]
    first = jnp.where(core == 0, keep, got)
    second = jnp.where(core == 0, got, keep)
    both = (first * jnp.exp(-rows * rates) + second).astype(bf16)
    groups = [list(range(c, ctx_count, 2)) for c in range(2)]
    spread = lax.all_to_all(
        jnp.broadcast_to(both, (ctx_count // 2, half, LANES)),
        "ctx",
        0,
        0,
        axis_index_groups=groups,
    )

    columns = jax.ShapeDtypeStruct((channels, width), bf16)
    query, base, steps, scale, *weights = pl.pallas_call(
        local_kernel,
        out_shape=(
            jax.ShapeDtypeStruct((rows, channels), bf16),
            jax.ShapeDtypeStruct((rows, channels), f32),
            state,
            state,
            columns,
            columns,
        ),
        in_specs=whole(1) + in_hbm(7),
        out_specs=tuple(whole(6)),
        scratch_shapes=[
            VMEM((rows, channels), bf16),
            VMEM((rows, channels), bf16),
            VMEM((order, channels), f32),
            VMEM((order, channels), f32),
            VMEM((1, channels), f32),
            VMEM((state_rows + 8, LANES), f32),
            VMEM((state_rows + 8, LANES), f32),
            VMEM((8 * rows + 8, LANES), f32),
            VMEM((8 * rows + 8, LANES), f32),
            pltpu.SemaphoreType.DMA((14,)),
        ],
        compiler_params=room(6),
        cost_estimate=pl.CostEstimate(flops=0, bytes_accessed=8 * 1024 * 1024, transcendentals=0),
        name="local_part",
    )(
        got,
        *fixed(
            key_feat,
            value_feat,
            decay_rate.T,
            residue.T,
            query_feat,
            conv_skip.reshape(1, channels),
            out_weight,
        ),
    )
    mine, other = pl.pallas_call(
        lambda *refs: carry_kernel(rows, *refs),
        out_shape=(state_half, state_half),
        in_specs=whole(4) + [pl.BlockSpec(memory_space=pl.ANY)],
        out_specs=tuple(whole(2)),
        compiler_params=room(4),
        name="carried_states",
    )(spread, keep, got, rates, steps)
    other = core_swap(other)

    piece = jax.ShapeDtypeStruct((rows, width), bf16)
    hyena, near, back = pl.pallas_call(
        gate_kernel,
        out_shape=(jax.ShapeDtypeStruct((rows, channels), bf16), piece, piece),
        in_specs=whole(8),
        out_specs=tuple(whole(3)),
        scratch_shapes=[VMEM((state_rows, LANES), f32), VMEM((8 * rows + 8, LANES), f32)],
        compiler_params=room(4),
        name="gate",
    )(query, base, steps, scale, mine, other, *weights)
    far = shifted(hyena, "chan", 2)
    near = shifted(near, "chan", 1)
    back = shifted(back, "chan", 3)

    attended, own, far_weight = pl.pallas_call(
        attention_kernel,
        out_shape=(
            jax.ShapeDtypeStruct(attn_query.shape, bf16),
            jax.ShapeDtypeStruct((rows, width), f32),
            columns,
        ),
        in_specs=in_hbm(9) + whole(2) + [pl.BlockSpec(memory_space=pltpu.SMEM)],
        out_specs=tuple(whole(3)),
        scratch_shapes=[VMEM(attn_query.shape, bf16)]
        + [VMEM((2 * rows, attn_query.shape[1]), bf16)] * 4
        + [
            VMEM((channels, width), bf16),
            VMEM((rows, width), bf16),
            pltpu.SemaphoreType.DMA((4, 5)),
            pltpu.SemaphoreType.DMA((7,)),
        ],
        compiler_params=room(8),
        name="attention",
    )(
        *fixed(attn_query, block, block_1, block_2, block_3),
        *fixed(out_weight, stream, far_half, far_other),
        hyena,
        doc_start.reshape(1, rows),
        read_mask,
    )
    mixed = pl.pallas_call(
        finish_kernel,
        out_shape=jax.ShapeDtypeStruct(stream.shape, bf16),
        in_specs=whole(5) + [pl.BlockSpec(memory_space=pl.ANY)],
        out_specs=in_hbm(1)[0],
        scratch_shapes=[VMEM(stream.shape, bf16), pltpu.SemaphoreType.DMA((4,))],
        compiler_params=room(4),
        name="finish",
    )(own, near, back, far, far_weight, *fixed(attended))
    return (mixed, attended)


def solution(mesh):
    in_specs = (
        P("ctx", "chan"),
        P("ctx", "chan"),
        P("ctx", "chan"),
        P("chan", None),
        P("chan", None),
        P("chan"),
        P("chan", None),
        P("ctx", "chan"),
        P("ctx", "chan"),
        P("ctx", "chan"),
        P("ctx", "chan"),
        P("ctx"),
        P("ctx", None),
    )
    out_specs = (P("ctx", "chan"), P("ctx", "chan"))
    return jax.shard_map(shards, mesh=mesh, in_specs=in_specs, out_specs=out_specs, check_vma=False)
```
